32 devices in a mesh: patch: 2 (over y), exp: 4 (over z), tile: 2 (over x), band: 2 (over core).
Axes of the slice: x: 2, y: 2, z: 4, core: 2. Of those that a mesh axis runs over, the one named last changes fastest.
Arguments:
- images: bfloat16 [4, 2, 64, 128, 128], P(('patch', 'band'), 'tile', 'exp'), parts along dimension 0, may hold values from -6 to 6
- mask_bits: int32 [4, 2, 64, 128, 128], P(('patch', 'band'), 'tile', 'exp'), parts along dimension 0, may hold values from 0 to 7
- inv_var: float32 [4, 2, 64], P(('patch', 'band'), 'tile', 'exp'), parts along dimension 0, may hold values from 0.5 to 4
- routes: int32 [4, 2, 64, 1], P(('patch', 'band'), 'tile', 'exp'), parts along dimension 0, may hold values from 0 to 3; in each aligned block of 16 rows (0 to 15, 16 to 31, ..., all dimensions but the last counted through in order) at most 8 rows name the same one
- block_slot: int32 [4, 2, 64], P(('patch', 'band'), 'tile', 'exp'), parts along dimension 0, may hold values from 0 to 7
- kernel_index: int32 [4, 2, 64], P(('patch', 'band'), 'tile', 'exp'), parts along dimension 0, may hold values from 0 to 63
- coefficients: float32 [64, 3], replicated, may hold values from -4 to 4
Outputs:
- coadd: float32 [4, 512, 2048], P(('patch', 'band'), 'tile', 'exp'), parts along dimension 0
- detection: float32 [1024, 2048], P(('patch', 'tile'), 'exp'), parts along dimension 0
The draws below stay inside these ranges and needn't reach their ends.
There are 2 independent parts, one for each index of `patch`. The reference program is written for one: setup_inputs(seed, part) draws one part's arguments, and reference() takes and returns one part's arrays. A program takes and returns all parts, laid end to end along the dimension named above; an argument that names none is the same for every part. Nothing has to cross between parts.
Inputs may be any that keep to these rules, and one draw needn't show every extreme that they name: Among the 16 sub-blocks of one device for one band and strip (an aligned block of routes), no tile column is named more than 8 times, and some tile column is named exactly 8 times.
All inputs are finite; a program needn't handle non-finite values.
Results may differ from the reference program's by a relative error of at most 0.0039.
Values may be sent and summed in bfloat16 or wider, within the bound.
No kernel may reach another device: no remote copies, remote signals or barrier semaphores. Data moves between devices by JAX's collectives and lax.ppermute only.
A program may use at most 128 MiB of HBM per device.

```python
import math
import jax
import jax.numpy as jnp
import numpy as np
from jax import lax

BLOCK = 128
TAPS = 41
NCOEF = 64
SB = 16
BLOCK_ROWS = 2
BLOCK_COLS = 4
CAP = 8
SUBS = 64
STRIPS = 2
BANDS = 2
N_EXP = 4


def touch_ends(values, own_key, low, top_value):
    extent = values.shape
    index_at = [jax.random.randint(jax.random.fold_in(own_key, axis), (), 0, extent[axis]) for axis in range(len(extent))]
    values = values.at[tuple(index_at)].set(low)
    longest = extent.index(max(extent))
    index_at[longest] = (index_at[longest] + 1) % extent[longest]
    return values.at[tuple(index_at)].set(top_value)


def levels(stream_key, shape, shards, least, largest):
    loudness = 1.0
    for dim, blocks in shards:
        draws = jax.random.uniform(jax.random.fold_in(jax.random.fold_in(stream_key, 6), dim), (blocks,), jnp.float32, least / len(shards), largest / len(shards))
        loudness = loudness * jnp.repeat(jnp.exp(draws), shape[dim] // blocks).reshape((-1,) + (1,) * (len(shape) - 1 - dim))
    return loudness


def routed_block(own_key, own, number, rows, amount, top, limit, skew):
    ranking = jax.random.permutation(own_key, amount)
    packed, common = load_shares(amount, rows * top, limit, skew, True), load_shares(amount, rows * top, limit, skew, False)
    places = jnp.arange(amount)

    def named(lengths, offset_by):
        used = int((lengths > 0).sum())
        fixed = max(1, used // 4)
        moved = fixed + (places - fixed + offset_by * (used - fixed)) % max(1, amount - fixed)
        return jnp.zeros((amount,), jnp.int32).at[ranking[jnp.where(places < fixed, places, moved)]].set(jnp.asarray(lengths, jnp.int32))

    lengths = jnp.where(number % 4 == 0, named(packed, number // 4), named(common, number - number // 4 - 1))
    mixed = jax.random.permutation(jax.random.fold_in(own, 3), amount)
    source_of, taker = mixed[0:amount // 2 * 2:2], mixed[1:amount // 2 * 2:2]
    slack = jnp.minimum(lengths[source_of] - 1, limit - lengths[taker]) // 2
    slack = jnp.where((source_of == ranking[0]) | (taker == ranking[0]) | (lengths[taker] == 0), 0, jnp.maximum(slack, 0))
    moved = jax.random.randint(jax.random.fold_in(own, 4), (amount // 2,), 0, 1 << 20) % (slack + 1)
    lengths = lengths.at[source_of].add(-moved).at[taker].add(moved)
    items = jnp.searchsorted(jnp.cumsum(lengths), jnp.arange(rows * top), side="right").astype(jnp.int32)
    table = items.reshape(top, rows).T
    table = table[jax.random.permutation(jax.random.fold_in(own, 1), rows)]
    offset_by = jax.random.randint(jax.random.fold_in(own, 2), (rows, 1), 0, top)
    return jnp.take_along_axis(table, (jnp.arange(top)[None, :] + offset_by) % top, axis=1)


def load_shares(number_of, total, most, skew, full):
    weights = [(1 << 20) // math.isqrt(rank ** skew) + 1 for rank in range(1, number_of + 1)]
    largest = most if full else min(most, max(-(-total // number_of), total * weights[0] // sum(weights)))
    least = 1 if total - largest >= number_of - 1 else 0
    holding, rest = [largest] + [least] * (number_of - 1), total - largest - least * (number_of - 1)
    while rest > 0:
        candidates = [i for i in range(1, number_of) if holding[i] < largest] or [i for i in range(1, number_of) if holding[i] < most]
        pool, left = sum([weights[i] for i in candidates]), rest
        for i in candidates:
            extra = min(most - holding[i], max(1, left * weights[i] // pool), rest)
            holding[i] = holding[i] + extra
            rest = rest - extra
    return np.array(holding)


def noise(key, dims, scale, limit, pieces=(), kind=jnp.bfloat16):
    factor_of = levels(key, dims, pieces, -0.22, 0.18) if pieces else 1.0
    array = jax.random.normal(key, dims, jnp.float32) * scale * factor_of
    return jnp.minimum(jnp.maximum(array, -limit), limit).astype(kind)


def setup_inputs(seed: int = 0, part: int = 0) -> dict:
    arg_keys = jax.random.split(jax.random.key(seed), 8)
    own_keys = jax.random.split(jax.random.fold_in(arg_keys[7], part), 8)
    images = noise(own_keys[0], (BANDS, STRIPS, SUBS, BLOCK, BLOCK), 1.0, 6.0, ((0, 2), (1, 2), (2, 4)))
    mask_bits = touch_ends(jax.random.randint(own_keys[1], (BANDS, STRIPS, SUBS, BLOCK, BLOCK), 0, 8), jax.random.fold_in(own_keys[1], 1), 0, 7).astype(jnp.int32)
    inv_var = jnp.clip(jnp.exp(math.log(4.0) - 2.0794415 * jax.random.uniform(own_keys[2], (BANDS, STRIPS, SUBS), jnp.float32) ** levels(own_keys[2], (BANDS, STRIPS, SUBS), ((0, 2), (1, 2), (2, 4)), -0.2, 0.2)), 0.5, 4.0)
    routes_keys = jax.random.split(jax.random.fold_in(own_keys[3], 1), BANDS * STRIPS * SUBS // SB)
    routes_turns = jax.random.permutation(jax.random.fold_in(own_keys[3], 3), BANDS * STRIPS * SUBS // SB)
    routes = jax.vmap(lambda own, number: routed_block(jax.random.fold_in(own_keys[3], 2), own, number, SB, N_EXP, 1, CAP, 2))(routes_keys, routes_turns).reshape((BANDS, STRIPS, SUBS, 1))
    block_slot = touch_ends(jax.random.randint(own_keys[4], (BANDS, STRIPS, SUBS), 0, BLOCK_ROWS * BLOCK_COLS), jax.random.fold_in(own_keys[4], 1), 0, (BLOCK_ROWS * BLOCK_COLS) - 1).astype(jnp.int32)
    kernel_index = touch_ends(jax.random.randint(own_keys[5], (BANDS, STRIPS, SUBS), 0, NCOEF), jax.random.fold_in(own_keys[5], 1), 0, NCOEF - 1).astype(jnp.int32)
    coefficients = noise(arg_keys[6], (NCOEF, 3), 1.0, 4.0, (), jnp.float32)
    return dict(images=images, mask_bits=mask_bits, inv_var=inv_var, routes=routes, block_slot=block_slot, kernel_index=kernel_index, coefficients=coefficients)


kernel_sigmas = (1.0, 2.5, 6.0)


def usable_share(bits):
    flagged = jnp.bitwise_and(bits, 6) == 6
    suspect = jnp.bitwise_and(bits, 1).astype(jnp.float32)
    return jnp.where(flagged, 0.0, 1.0 - 0.5 * suspect).astype(jnp.float32)


def gaussian_taps(half_span):
    taps_axis = jnp.arange(-half_span, half_span + 1).astype(jnp.float32)
    result = []
    for spread in kernel_sigmas:
        values = jnp.exp(-taps_axis * taps_axis / (2.0 * spread * spread))
        result.append(values / jnp.sum(values))
    return jnp.stack(result)


def to_image(blocks):
    grid_rows, grid_cols = blocks.shape[0], blocks.shape[1]
    return blocks.transpose(0, 2, 1, 3).reshape(grid_rows * BLOCK, grid_cols * BLOCK)


def reference(images, mask_bits, inv_var, routes, block_slot, kernel_index, coefficients):
    half_span = TAPS // 2
    taps = gaussian_taps(half_span)
    grid_rows = STRIPS * BLOCK_ROWS
    grid_cols = N_EXP * BLOCK_COLS
    strip_of = jnp.repeat(jnp.arange(STRIPS, dtype=jnp.int32), SUBS)
    coadds = []
    detection = jnp.zeros((grid_rows * BLOCK, grid_cols * BLOCK), jnp.float32)
    for band_index in range(BANDS):
        usable = usable_share(mask_bits[band_index].reshape(-1, BLOCK, BLOCK))
        inverse = inv_var[band_index].reshape(-1)[:, None, None]
        weight = (usable * inverse).astype(jnp.bfloat16)
        pictures = images[band_index].reshape(-1, BLOCK, BLOCK).astype(jnp.float32)
        weighted = (usable * inverse * pictures).astype(jnp.bfloat16)
        slot_here = block_slot[band_index].reshape(-1).astype(jnp.int32)
        owner = routes[band_index].reshape(-1).astype(jnp.int32)
        block_row = (strip_of * BLOCK_ROWS + slot_here // BLOCK_COLS).astype(jnp.int32)
        block_col = (owner * BLOCK_COLS + slot_here % BLOCK_COLS).astype(jnp.int32)
        coef_rows = coefficients[kernel_index[band_index].reshape(-1).astype(jnp.int32)]
        empty = jnp.zeros((grid_rows, grid_cols, BLOCK, BLOCK), jnp.float32)
        planes = []
        for basis_index in range(3):
            contrib = coef_rows[:, basis_index][:, None, None] * weighted.astype(jnp.float32)
            planes.append(to_image(empty.at[block_row, block_col].add(contrib)))
        depth_sum = to_image(empty.at[block_row, block_col].add(weight.astype(jnp.float32)))
        stacked = jnp.stack(planes)[None]
        downward = lax.conv_general_dilated(stacked, taps[:, None, :, None], (1, 1), ((half_span, half_span), (0, 0)), dimension_numbers=("NCHW", "OIHW", "NCHW"), feature_group_count=3, precision=lax.Precision.HIGHEST)
        sideways = lax.conv_general_dilated(downward, taps[:, None, None, :], (1, 1), ((0, 0), (half_span, half_span)), dimension_numbers=("NCHW", "OIHW", "NCHW"), feature_group_count=3, precision=lax.Precision.HIGHEST)
        matched = jnp.sum(sideways[0], axis=0)
        denominator = 1.0 + depth_sum
        coadded = matched / denominator
        coadds.append(coadded)
        detection = detection + coadded * coadded * denominator
    return jnp.stack(coadds), detection
```

```python
import functools

import jax
import jax.numpy as jnp
import ml_dtypes
import numpy as np
from jax import lax
from jax.experimental import pallas as pl
from jax.experimental.pallas import tpu as pltpu
from jax.sharding import PartitionSpec as P

BLOCK = 128
TAPS = 41
BLOCK_ROWS = 2
BLOCK_COLS = 4


kernel_sigmas = (1.0, 2.5, 6.0)


def extended(block, sides, width):
    for axis, dim in sides:
        count = lax.axis_size(axis)
        forward = [(i, i + 1) for i in range(count - 1)]
        backward = [(target, source) for source, target in forward]
        low = lax.ppermute(
            lax.slice_in_dim(block, block.shape[dim] - width, None, axis=dim), axis, forward
        )
        high = lax.ppermute(lax.slice_in_dim(block, 0, width, axis=dim), axis, backward)
        block = jnp.concatenate([low, block, high], axis=dim)
    return block


def usable_share(bits):
    flagged = jnp.bitwise_and(bits, 6) == 6
    suspect = jnp.bitwise_and(bits, 1).astype(jnp.float32)
    return jnp.where(flagged, 0.0, 1.0 - 0.5 * suspect)


def band_matrix(length, half_span):
    rows_here = jnp.arange(length + 2 * half_span, dtype=jnp.int32)[:, None]
    cols_here = jnp.arange(length, dtype=jnp.int32)[None, :]
    offset = (rows_here - cols_here - half_span).astype(jnp.float32)
    inside = jnp.abs(offset) <= half_span
    taps_axis = jnp.arange(-half_span, half_span + 1).astype(jnp.float32)
    result = []
    for spread in kernel_sigmas:
        norm_sum = jnp.sum(jnp.exp(-taps_axis * taps_axis / (2.0 * spread * spread)))
        result.append(
            jnp.where(inside, jnp.exp(-offset * offset / (2.0 * spread * spread)), 0.0) / norm_sum
        )
    return jnp.stack(result)


def routed(images, mask_bits, inv_var, routes, block_slot, kernel_index, coefficients):
    peer_count = lax.axis_size("exp")
    held_count = images.shape[2]
    capacity = max(2, 2 * held_count // peer_count)
    slot_count = peer_count * capacity
    pixels = BLOCK * BLOCK
    tile_blocks = BLOCK_ROWS * BLOCK_COLS
    coef_count = coefficients.shape[0]
    usable = usable_share(mask_bits[0, 0])
    inverse = inv_var[0, 0][:, None, None]
    weight = (usable * inverse).astype(jnp.bfloat16).reshape(held_count, pixels)
    weighted = (
        (usable * inverse * images[0, 0].astype(jnp.float32))
        .astype(jnp.bfloat16)
        .reshape(held_count, pixels)
    )
    target = routes[0, 0, :, 0]
    ordinal = jnp.arange(held_count, dtype=jnp.int32)
    same_target = target[:, None] == target[None, :]
    earlier = jnp.sum(
        (same_target & (ordinal[None, :] < ordinal[:, None])).astype(jnp.int32), axis=1
    )
    position = target * capacity + earlier
    placed = jnp.arange(slot_count, dtype=jnp.int32)[:, None] == position[None, :]
    placed_int = placed.astype(jnp.int32)
    slot_block = jnp.sum(placed_int * (block_slot[0, 0] + 1)[None, :], axis=1) - 1
    slot_kernel = jnp.sum(placed_int * kernel_index[0, 0][None, :], axis=1)
    labels = jnp.stack([slot_block, slot_kernel], axis=1).reshape(peer_count, capacity, 2)
    placed_half = placed.astype(jnp.bfloat16)
    send_weight = (
        jnp.dot(placed_half, weight, preferred_element_type=jnp.float32)
        .astype(jnp.bfloat16)
        .reshape(peer_count, capacity, pixels)
    )
    block_ids = jnp.arange(tile_blocks, dtype=jnp.int32)[:, None]
    send_weighted = (
        jnp.dot(placed_half, weighted, preferred_element_type=jnp.float32)
        .astype(jnp.bfloat16)
        .reshape(peer_count, capacity, pixels)
    )
    got_weighted, got_weight, got_labels = (
        lax.all_to_all(send_weighted, "exp", split_axis=0, concat_axis=0, tiled=True),
        lax.all_to_all(send_weight, "exp", split_axis=0, concat_axis=0, tiled=True),
        lax.all_to_all(labels, "exp", split_axis=0, concat_axis=0, tiled=True),
    )
    got_labels = got_labels.reshape(slot_count, 2)
    into_block = block_ids == got_labels[:, 0][None, :]
    kernel_pick = (
        got_labels[:, 1][:, None] == jnp.arange(coef_count, dtype=jnp.int32)[None, :]
    ).astype(jnp.float32)
    slot_mix = jnp.dot(kernel_pick, coefficients, precision=lax.Precision.HIGHEST)
    mixing = slot_mix.T[:, None, :] * into_block.astype(jnp.float32)[None, :, :]
    basis_sum = jnp.einsum(
        "kbp,px->kbx",
        mixing,
        got_weighted.reshape(slot_count, pixels).astype(jnp.float32),
        precision=lax.Precision.HIGHEST,
    )
    depth_sum = jnp.dot(
        into_block.astype(jnp.bfloat16),
        got_weight.reshape(slot_count, pixels),
        preferred_element_type=jnp.float32,
    )
    tile_rows = BLOCK_ROWS * BLOCK
    tile_cols = BLOCK_COLS * BLOCK
    basis_tile = (
        basis_sum.reshape(3, BLOCK_ROWS, BLOCK_COLS, BLOCK, BLOCK)
        .transpose(0, 1, 3, 2, 4)
        .reshape(3, tile_rows, tile_cols)
    )
    depth_tile = (
        depth_sum.reshape(BLOCK_ROWS, BLOCK_COLS, BLOCK, BLOCK)
        .transpose(0, 2, 1, 3)
        .reshape(tile_rows, tile_cols)
    )
    half_span = TAPS // 2
    column_mix = band_matrix(tile_cols, half_span)
    row_mix = band_matrix(tile_rows, half_span).transpose(0, 2, 1)
    framed = extended(basis_tile, (("exp", 2), ("tile", 1)), half_span)
    across = jnp.einsum("kyp,kpc->kyc", framed, column_mix, precision=lax.Precision.HIGHEST)
    matched = jnp.einsum("kry,kyc->rc", row_mix, across, precision=lax.Precision.HIGHEST)
    denominator = 1.0 + depth_tile
    coadded = matched / denominator
    detection = lax.psum(coadded * coadded * denominator, "band")
    return (coadded[None], detection)


HALF = TAPS // 2
EDGE = 32
REACH = 152
LINE = 4
TILE_BLOCKS = BLOCK_ROWS * BLOCK_COLS
TILE_ROWS = BLOCK_ROWS * BLOCK
TILE_COLS = BLOCK_COLS * BLOCK
MEBI = 1024 * 1024


def tap_values(offset):
    span = np.arange(-HALF, HALF + 1, dtype=np.float64)
    inside = np.abs(offset) <= HALF
    result = []
    for spread in kernel_sigmas:
        total = np.exp(-span * span / (2.0 * spread * spread)).sum()
        value = np.exp(-offset.astype(np.float64) ** 2 / (2.0 * spread * spread)) / total
        result.append(np.where(inside, value, 0.0))
    return np.stack(result)


def split_taps(values):
    high = values.astype(ml_dtypes.bfloat16)
    low = (values - high.astype(np.float64)).astype(ml_dtypes.bfloat16)
    return high, low


def row_taps(first_row, rows):
    result = []
    for block_row in range(BLOCK_ROWS):
        target = first_row[block_row] + np.arange(rows)[:, None]
        source = block_row * BLOCK + np.arange(BLOCK)[None, :]
        values = tap_values(target - source).reshape(3 * rows, BLOCK)
        result.append(np.concatenate(split_taps(values), axis=1))
    return np.stack(result)


def column_taps():
    lane = np.arange(BLOCK)
    beside = np.where(lane < BLOCK // 2, lane + BLOCK, lane - BLOCK)
    target = np.concatenate([lane, beside])[None, :]
    high, low = split_taps(tap_values(target - lane[:, None]).reshape(3 * BLOCK, 2 * BLOCK))
    return np.concatenate([high, high, low], axis=0)


def code(value):
    return (value * jnp.abs(value)).astype(jnp.bfloat16)


def decode(coded):
    square = coded.astype(jnp.float32)
    root = jnp.sqrt(jnp.abs(square))
    return jnp.where(square < 0, -root, root)


def tile_at(place):
    me = lax.axis_index("exp")
    return jnp.where(me < LINE // 2, LINE - 1 - place, place)


def split_rows(block, mixing):
    rows = block.shape[0] // 3
    high, low = [], []
    for k in range(3):
        value = mixing[k] * block[k * rows : (k + 1) * rows]
        rounded = value.astype(jnp.bfloat16)
        high.append(rounded)
        low.append((value - rounded.astype(jnp.float32)).astype(jnp.bfloat16))
    return jnp.concatenate(high + low + high, axis=1)


def spread_columns(target, column, rows, values):
    beside = values[:, BLOCK:]
    to_right = lax.broadcasted_iota(jnp.int32, beside.shape, 1) < BLOCK // 2
    target[column, rows] += values[:, :BLOCK]
    target[column + 1, rows] += jnp.where(to_right, beside, 0.0)
    target[column - 1, rows] += jnp.where(to_right, 0.0, beside)


def pixel_kernel(held, *refs):
    (
        routes_in, slots_in, inverse_in, bits_in, images_in,
        out_weighted, out_far, out_third, out_last,
        routes, slots, inverse, bits, images, share, depth, far, sems,
    ) = refs
    small = [
        pltpu.make_async_copy(src, dst, sems.at[n])
        for n, (src, dst) in enumerate(
            ((routes_in, routes), (slots_in, slots), (inverse_in, inverse))
        )
    ]
    parts = 4
    size = held // parts
    large = [
        pltpu.make_async_copy(
            src.at[pl.ds(p * size, size)], dst.at[pl.ds(p * size, size)], sems.at[3 + first + p]
        )
        for first, src, dst in ((0, bits_in, bits), (parts, images_in, images))
        for p in range(parts)
    ]
    for copy in small + large:
        copy.start()
    depth[...] = jnp.zeros_like(depth)
    for copy in small:
        copy.wait()
    for s in range(held):
        if s % size == 0:
            large[s // size].wait()
        flags = bits[s]
        full = inverse[s]
        part = jnp.where((flags & 1) == 1, 0.5 * full, full)
        part = jnp.where((flags & 6) == 6, 0.0, part)
        share[s] = part
        depth[routes[s] * TILE_BLOCKS + slots[s]] += part.astype(jnp.bfloat16).astype(jnp.float32)

    def write_depth(place, ref):
        tile = tile_at(place)
        for b in range(TILE_BLOCKS):
            row, col = b // BLOCK_COLS * BLOCK, b % BLOCK_COLS * BLOCK
            ref[row : row + BLOCK, col : col + BLOCK] = depth[tile * TILE_BLOCKS + b].astype(
                jnp.bfloat16
            )

    for place in range(2):
        write_depth(place, far.at[place])
    out_copy = pltpu.make_async_copy(far, out_far, sems.at[3 + 2 * parts])
    out_copy.start()
    write_depth(2, out_third)
    write_depth(3, out_last)
    for s in range(held):
        if s % size == 0:
            large[parts + s // size].wait()
        out_weighted[s] = (share[s] * images[s].astype(jnp.float32)).astype(jnp.bfloat16)
    out_copy.wait()


def edge_kernel(held, routes, slots, kinds, coefs, weighted, taps, col_taps, out_edge, factors, total):
    strip = lax.axis_index("tile")
    total[...] = jnp.zeros_like(total)
    for s in range(held):
        pixels = weighted[s]
        moved = jnp.dot(
            taps[1 - strip],
            jnp.concatenate([pixels, pixels], axis=0),
            preferred_element_type=jnp.float32,
        )
        crosses = (slots[s] // BLOCK_COLS == 1 - strip).astype(jnp.float32)
        factors[s * EDGE : (s + 1) * EDGE] = split_rows(
            moved, [crosses * coefs[k, kinds[s]] for k in range(3)]
        )
    result = jnp.dot(factors[...], col_taps[...], preferred_element_type=jnp.float32)
    for s in range(held):
        column = 1 + routes[s] * BLOCK_COLS + slots[s] % BLOCK_COLS
        spread_columns(total, column, pl.ds(0, EDGE), result[s * EDGE : (s + 1) * EDGE])
    for place in range(LINE):
        for b in range(BLOCK_COLS):
            out_edge[place, :, b * BLOCK : (b + 1) * BLOCK] = total[
                1 + tile_at(place) * BLOCK_COLS + b
            ].astype(jnp.bfloat16)


def match_kernel(held, *refs):
    routes, slots, kinds, coefs, weighted, taps, col_taps = refs[:7]
    out_tiles = refs[7 : 7 + LINE]
    total = refs[7 + LINE]
    total[...] = jnp.zeros_like(total)
    for s in range(held):
        slot = slots[s]
        block_row = slot // BLOCK_COLS
        pixels = weighted[s]
        moved = jnp.dot(
            taps[block_row],
            jnp.concatenate([pixels, pixels], axis=0),
            preferred_element_type=jnp.float32,
        )
        factors = split_rows(moved, [coefs[k, kinds[s]] for k in range(3)])
        result = jnp.dot(factors, col_taps[...], preferred_element_type=jnp.float32)
        row = pl.multiple_of(block_row * (TILE_ROWS - REACH), 8)
        column = 1 + routes[s] * BLOCK_COLS + slot % BLOCK_COLS
        spread_columns(total, column, pl.ds(row, REACH), result)
    for place in range(LINE):
        for b in range(BLOCK_COLS):
            out_tiles[place][:, b * BLOCK : (b + 1) * BLOCK] = total[
                1 + tile_at(place) * BLOCK_COLS + b
            ]


def edge_rows():
    return pl.ds(pl.multiple_of((1 - lax.axis_index("tile")) * (TILE_ROWS - EDGE), EDGE), EDGE)


def relay_kernel(own, got, edge, out):
    rows = edge_rows()
    out[...] = code(own[...] + decode(got[...]))
    out[rows] = code(own[rows] + edge[...].astype(jnp.float32) + decode(got[rows]))


def final_kernel(
    third_d, last_d, got_third, got_far_d, got_last_d, third_m, last_m, edge, got_m, got_last_m,
    out_coadd, out_term, total,
):
    me = lax.axis_index("exp")
    at_end = jnp.logical_or(me == 0, me == LINE - 1)
    own_m = jnp.where(at_end, last_m[...], third_m[...])
    total[...] = own_m + decode(got_third[1]) + (decode(got_m[...]) + decode(got_last_m[...]))
    rows = edge_rows()
    total[rows] += jnp.where(at_end, edge[3].astype(jnp.float32), edge[2].astype(jnp.float32))
    own_d = jnp.where(at_end, last_d[...].astype(jnp.float32), third_d[...].astype(jnp.float32))
    denominator = (
        (1.0 + own_d)
        + got_third[0].astype(jnp.float32)
        + (got_far_d[1].astype(jnp.float32) + got_last_d[...].astype(jnp.float32))
    )
    coadd = total[...] / denominator
    out_coadd[...] = coadd
    out_term[...] = (coadd * coadd * denominator).astype(jnp.bfloat16)


def first_kernel(tile_0, tile_1, tile_2, edge, third_d, far, next_far, third_both):
    rows = edge_rows()
    for place, (source, out) in enumerate(((tile_0, far), (tile_1, next_far), (tile_2, third_both.at[1]))):
        out[...] = code(source[...])
        out[rows] = code(source[rows] + edge[place].astype(jnp.float32))
    third_both[0] = third_d[...]


def in_vmem(count):
    return [pl.BlockSpec(memory_space=pltpu.VMEM)] * count


def in_smem(count):
    return [pl.BlockSpec(memory_space=pltpu.SMEM)] * count


def in_hbm(count):
    return [pl.BlockSpec(memory_space=pltpu.HBM)] * count


def vmem_limit(mebibytes):
    return pltpu.CompilerParams(vmem_limit_bytes=mebibytes * MEBI)


def reduced(images, mask_bits, inv_var, routes, block_slot, kernel_index, coefficients):
    held = images.shape[2]
    tile = jax.ShapeDtypeStruct((TILE_ROWS, TILE_COLS), jnp.bfloat16)
    wide = jax.ShapeDtypeStruct((TILE_ROWS, TILE_COLS), jnp.float32)
    pair = jax.ShapeDtypeStruct((2, TILE_ROWS, TILE_COLS), jnp.bfloat16)
    columns = LINE * BLOCK_COLS + 2
    target, slot, kind = routes.reshape(held), block_slot.reshape(held), kernel_index.reshape(held)
    mixing = coefficients.T
    inward = [(0, 1), (LINE - 1, LINE - 2)]
    across = [(1, 2), (2, 1)]
    outward = [(1, 0), (LINE - 2, LINE - 1)]

    weighted, far_d, third_d, last_d = pl.pallas_call(
        functools.partial(pixel_kernel, held),
        out_shape=[jax.ShapeDtypeStruct((held, BLOCK, BLOCK), jnp.bfloat16), pair, tile, tile],
        in_specs=in_hbm(5),
        out_specs=in_vmem(1) + in_hbm(1) + in_vmem(2),
        scratch_shapes=[
            pltpu.SMEM((held,), jnp.int32),
            pltpu.SMEM((held,), jnp.int32),
            pltpu.SMEM((held,), jnp.float32),
            pltpu.VMEM((held, BLOCK, BLOCK), jnp.int32),
            pltpu.VMEM((held, BLOCK, BLOCK), jnp.bfloat16),
            pltpu.VMEM((held, BLOCK, BLOCK), jnp.float32),
            pltpu.VMEM((LINE * TILE_BLOCKS, BLOCK, BLOCK), jnp.float32),
            pltpu.VMEM((2, TILE_ROWS, TILE_COLS), jnp.bfloat16),
            pltpu.SemaphoreType.DMA((12,)),
        ],
        compiler_params=vmem_limit(24),
        name="pixels",
    )(target, slot, inv_var.reshape(held), mask_bits[0, 0], images[0, 0])
    got_far_d = lax.ppermute(far_d, "exp", inward)

    col_taps = jnp.asarray(column_taps())
    edge = pl.pallas_call(
        functools.partial(edge_kernel, held),
        out_shape=jax.ShapeDtypeStruct((LINE, EDGE, TILE_COLS), jnp.bfloat16),
        in_specs=in_smem(4) + in_vmem(3),
        out_specs=pl.BlockSpec(memory_space=pltpu.VMEM),
        scratch_shapes=[
            pltpu.VMEM((held * EDGE, 9 * BLOCK), jnp.bfloat16),
            pltpu.VMEM((columns, EDGE, BLOCK), jnp.float32),
        ],
        compiler_params=vmem_limit(24),
        name="edges",
    )(target, slot, kind, mixing, weighted, jnp.asarray(row_taps((-EDGE, TILE_ROWS), EDGE)), col_taps)
    other_edge = lax.ppermute(edge, "tile", [(0, 1), (1, 0)])

    own_m = pl.pallas_call(
        functools.partial(match_kernel, held),
        out_shape=[wide] * LINE,
        in_specs=in_smem(4) + in_vmem(3),
        out_specs=in_vmem(LINE),
        scratch_shapes=[pltpu.VMEM((columns, TILE_ROWS, BLOCK), jnp.float32)],
        compiler_params=vmem_limit(24),
        name="match",
    )(target, slot, kind, mixing, weighted, jnp.asarray(row_taps((0, TILE_ROWS - REACH), REACH)), col_taps)
    far_m, next_m, third_both = pl.pallas_call(
        first_kernel,
        out_shape=[tile, tile, pair],
        in_specs=in_vmem(5),
        out_specs=in_vmem(3),
        compiler_params=vmem_limit(24),
        name="first",
    )(*own_m[:3], other_edge, third_d)

    def relay(own, got, place):
        return pl.pallas_call(
            relay_kernel,
            out_shape=tile,
            in_specs=in_vmem(3),
            out_specs=pl.BlockSpec(memory_space=pltpu.VMEM),
            compiler_params=vmem_limit(24),
            name="relay",
        )(own, got, other_edge[place])

    got_far_m = lax.ppermute(far_m, "exp", inward)
    mid_d = lax.ppermute(far_d + got_far_d, "exp", across)
    got_next_m = lax.ppermute(next_m, "exp", inward)
    mid_far_m = lax.ppermute(relay(own_m[0], got_far_m, 0), "exp", across)
    got_third = lax.ppermute(third_both, "exp", inward)
    end_d = lax.ppermute(last_d + mid_d[0], "exp", outward)
    mid_m = lax.ppermute(relay(own_m[1], got_next_m, 1), "exp", across)
    end_m = lax.ppermute(relay(own_m[3], mid_far_m, 3), "exp", outward)
    coadd, term = pl.pallas_call(
        final_kernel,
        out_shape=[wide, tile],
        in_specs=in_vmem(10),
        out_specs=in_vmem(2),
        scratch_shapes=[pltpu.VMEM((TILE_ROWS, TILE_COLS), jnp.float32)],
        compiler_params=vmem_limit(24),
        name="final",
    )(third_d, last_d, got_third, mid_d, end_d, own_m[2], own_m[3], other_edge, mid_m, end_m)
    other_term = lax.ppermute(term, "band", [(0, 1), (1, 0)])
    detection = term.astype(jnp.float32) + other_term.astype(jnp.float32)
    return (coadd[None], detection)


def local(images, mask_bits, inv_var, routes, block_slot, kernel_index, coefficients):
    peers = lax.axis_size("exp")
    partial_sums_fit = peers * TILE_BLOCKS <= 2 * images.shape[2]
    pairs = lax.axis_size("tile") == 2 and lax.axis_size("band") == 2
    plan = reduced if partial_sums_fit and pairs and peers == LINE else routed
    return plan(images, mask_bits, inv_var, routes, block_slot, kernel_index, coefficients)


def solution(mesh):
    return jax.shard_map(
        local,
        mesh=mesh,
        in_specs=(
            P(("patch", "band"), "tile", "exp", None, None),
            P(("patch", "band"), "tile", "exp", None, None),
            P(("patch", "band"), "tile", "exp"),
            P(("patch", "band"), "tile", "exp", None),
            P(("patch", "band"), "tile", "exp"),
            P(("patch", "band"), "tile", "exp"),
            P(),
        ),
        out_specs=(P(("patch", "band"), "tile", "exp"), P(("patch", "tile"), "exp")),
        check_vma=False,
    )
```

```python
import functools

import jax
import jax.numpy as jnp
import ml_dtypes
import numpy as np
from jax import lax
from jax.experimental import pallas as pl
from jax.experimental.pallas import tpu as pltpu
from jax.sharding import PartitionSpec as P

BLOCK = 128
TAPS = 41
BLOCK_ROWS = 2
BLOCK_COLS = 4


kernel_sigmas = (1.0, 2.5, 6.0)


def extended(block, sides, width):
    for axis, dim in sides:
        count = lax.axis_size(axis)
        forward = [(i, i + 1) for i in range(count - 1)]
        backward = [(target, source) for source, target in forward]
        low = lax.ppermute(
            lax.slice_in_dim(block, block.shape[dim] - width, None, axis=dim), axis, forward
        )
        high = lax.ppermute(lax.slice_in_dim(block, 0, width, axis=dim), axis, backward)
        block = jnp.concatenate([low, block, high], axis=dim)
    return block


def usable_share(bits):
    flagged = jnp.bitwise_and(bits, 6) == 6
    suspect = jnp.bitwise_and(bits, 1).astype(jnp.float32)
    return jnp.where(flagged, 0.0, 1.0 - 0.5 * suspect)


def band_matrix(length, half_span):
    rows_here = jnp.arange(length + 2 * half_span, dtype=jnp.int32)[:, None]
    cols_here = jnp.arange(length, dtype=jnp.int32)[None, :]
    offset = (rows_here - cols_here - half_span).astype(jnp.float32)
    inside = jnp.abs(offset) <= half_span
    taps_axis = jnp.arange(-half_span, half_span + 1).astype(jnp.float32)
    result = []
    for spread in kernel_sigmas:
        norm_sum = jnp.sum(jnp.exp(-taps_axis * taps_axis / (2.0 * spread * spread)))
        result.append(
            jnp.where(inside, jnp.exp(-offset * offset / (2.0 * spread * spread)), 0.0) / norm_sum
        )
    return jnp.stack(result)


def routed(images, mask_bits, inv_var, routes, block_slot, kernel_index, coefficients):
    peer_count = lax.axis_size("exp")
    held_count = images.shape[2]
    capacity = max(2, 2 * held_count // peer_count)
    slot_count = peer_count * capacity
    pixels = BLOCK * BLOCK
    tile_blocks = BLOCK_ROWS * BLOCK_COLS
    coef_count = coefficients.shape[0]
    usable = usable_share(mask_bits[0, 0])
    inverse = inv_var[0, 0][:, None, None]
    weight = (usable * inverse).astype(jnp.bfloat16).reshape(held_count, pixels)
    weighted = (
        (usable * inverse * images[0, 0].astype(jnp.float32))
        .astype(jnp.bfloat16)
        .reshape(held_count, pixels)
    )
    target = routes[0, 0, :, 0]
    ordinal = jnp.arange(held_count, dtype=jnp.int32)
    same_target = target[:, None] == target[None, :]
    earlier = jnp.sum(
        (same_target & (ordinal[None, :] < ordinal[:, None])).astype(jnp.int32), axis=1
    )
    position = target * capacity + earlier
    placed = jnp.arange(slot_count, dtype=jnp.int32)[:, None] == position[None, :]
    placed_int = placed.astype(jnp.int32)
    slot_block = jnp.sum(placed_int * (block_slot[0, 0] + 1)[None, :], axis=1) - 1
    slot_kernel = jnp.sum(placed_int * kernel_index[0, 0][None, :], axis=1)
    labels = jnp.stack([slot_block, slot_kernel], axis=1).reshape(peer_count, capacity, 2)
    placed_half = placed.astype(jnp.bfloat16)
    send_weight = (
        jnp.dot(placed_half, weight, preferred_element_type=jnp.float32)
        .astype(jnp.bfloat16)
        .reshape(peer_count, capacity, pixels)
    )
    block_ids = jnp.arange(tile_blocks, dtype=jnp.int32)[:, None]
    send_weighted = (
        jnp.dot(placed_half, weighted, preferred_element_type=jnp.float32)
        .astype(jnp.bfloat16)
        .reshape(peer_count, capacity, pixels)
    )
    got_weighted, got_weight, got_labels = (
        lax.all_to_all(send_weighted, "exp", split_axis=0, concat_axis=0, tiled=True),
        lax.all_to_all(send_weight, "exp", split_axis=0, concat_axis=0, tiled=True),
        lax.all_to_all(labels, "exp", split_axis=0, concat_axis=0, tiled=True),
    )
    got_labels = got_labels.reshape(slot_count, 2)
    into_block = block_ids == got_labels[:, 0][None, :]
    kernel_pick = (
        got_labels[:, 1][:, None] == jnp.arange(coef_count, dtype=jnp.int32)[None, :]
    ).astype(jnp.float32)
    slot_mix = jnp.dot(kernel_pick, coefficients, precision=lax.Precision.HIGHEST)
    mixing = slot_mix.T[:, None, :] * into_block.astype(jnp.float32)[None, :, :]
    basis_sum = jnp.einsum(
        "kbp,px->kbx",
        mixing,
        got_weighted.reshape(slot_count, pixels).astype(jnp.float32),
        precision=lax.Precision.HIGHEST,
    )
    depth_sum = jnp.dot(
        into_block.astype(jnp.bfloat16),
        got_weight.reshape(slot_count, pixels),
        preferred_element_type=jnp.float32,
    )
    tile_rows = BLOCK_ROWS * BLOCK
    tile_cols = BLOCK_COLS * BLOCK
    basis_tile = (
        basis_sum.reshape(3, BLOCK_ROWS, BLOCK_COLS, BLOCK, BLOCK)
        .transpose(0, 1, 3, 2, 4)
        .reshape(3, tile_rows, tile_cols)
    )
    depth_tile = (
        depth_sum.reshape(BLOCK_ROWS, BLOCK_COLS, BLOCK, BLOCK)
        .transpose(0, 2, 1, 3)
        .reshape(tile_rows, tile_cols)
    )
    half_span = TAPS // 2
    column_mix = band_matrix(tile_cols, half_span)
    row_mix = band_matrix(tile_rows, half_span).transpose(0, 2, 1)
    framed = extended(basis_tile, (("exp", 2), ("tile", 1)), half_span)
    across = jnp.einsum("kyp,kpc->kyc", framed, column_mix, precision=lax.Precision.HIGHEST)
    matched = jnp.einsum("kry,kyc->rc", row_mix, across, precision=lax.Precision.HIGHEST)
    denominator = 1.0 + depth_tile
    coadded = matched / denominator
    detection = lax.psum(coadded * coadded * denominator, "band")
    return (coadded[None], detection)


HALF = TAPS // 2
EDGE = 32
REACH = 24
LINE = 4
PARTS = 4
TILE_BLOCKS = BLOCK_ROWS * BLOCK_COLS
TILE_ROWS = BLOCK_ROWS * BLOCK
TILE_COLS = BLOCK_COLS * BLOCK
MEBI = 1024 * 1024


def tap_values(offset):
    span = np.arange(-HALF, HALF + 1, dtype=np.float64)
    inside = np.abs(offset) <= HALF
    result = []
    for spread in kernel_sigmas:
        total = np.exp(-span * span / (2.0 * spread * spread)).sum()
        value = np.exp(-offset.astype(np.float64) ** 2 / (2.0 * spread * spread)) / total
        result.append(np.where(inside, value, 0.0))
    return np.stack(result)


def split_taps(values):
    high = values.astype(ml_dtypes.bfloat16)
    low = (values - high.astype(np.float64)).astype(ml_dtypes.bfloat16)
    return high, low


def row_taps(target):
    values = tap_values(target[:, None] - np.arange(BLOCK)[None, :])
    return np.concatenate(split_taps(values.reshape(-1, BLOCK)), axis=1)


def tap_scales():
    values = tap_values(np.arange(-HALF, HALF + 1))[:, None, :]
    factors = np.linspace(1.0, 2.0, 4096, endpoint=False)[None, :, None]
    rounded = (values * factors).astype(ml_dtypes.bfloat16).astype(np.float64) / factors
    return factors[0, np.argmin(((rounded - values) ** 2).sum(axis=-1), axis=1), 0]


def column_taps():
    lane = np.arange(BLOCK)
    beside = np.where(lane < BLOCK // 2, lane + BLOCK, lane - BLOCK)
    target = np.concatenate([lane, beside])[None, :]
    values = tap_values(target - lane[:, None]) * tap_scales()[:, None, None]
    rounded = values.reshape(3 * BLOCK, 2 * BLOCK).astype(ml_dtypes.bfloat16)
    return np.concatenate([rounded, rounded], axis=0)


def code(value):
    return (value * jnp.abs(value)).astype(jnp.bfloat16)


def decode(coded):
    square = coded.astype(jnp.float32)
    root = jnp.sqrt(jnp.abs(square))
    return jnp.where(square < 0, -root, root)


def tile_at(place):
    me = lax.axis_index("exp")
    return jnp.where(me < LINE // 2, LINE - 1 - place, place)


def split_rows(block, mixing):
    rows = block.shape[0] // 3
    high, low = [], []
    for k in range(3):
        value = mixing[k] * block[k * rows : (k + 1) * rows]
        rounded = value.astype(jnp.bfloat16)
        high.append(rounded)
        low.append((value - rounded.astype(jnp.float32)).astype(jnp.bfloat16))
    return jnp.concatenate(high + low, axis=1)


def spread_columns(target, column, rows, values):
    beside = values[:, BLOCK:]
    to_right = lax.broadcasted_iota(jnp.int32, beside.shape, 1) < BLOCK // 2
    target[column, rows] += values[:, :BLOCK]
    target[column + 1, rows] += jnp.where(to_right, beside, 0.0)
    target[column - 1, rows] += jnp.where(to_right, 0.0, beside)


def pixel_share(flags, full):
    part = jnp.where((flags & 1) == 1, 0.5 * full, full)
    return jnp.where((flags & 6) == 6, 0.0, part)


def start_all(pairs, sems):
    copies = [pltpu.make_async_copy(src, dst, sems.at[n]) for n, (src, dst) in enumerate(pairs)]
    for copy in copies:
        copy.start()
    return copies


def in_parts(src, dst, parts):
    size = src.shape[0] // parts
    return [(src.at[pl.ds(p * size, size)], dst.at[pl.ds(p * size, size)]) for p in range(parts)]


def depth_kernel(held, *refs):
    routes_in, slots_in, inverse_in, bits_in = refs[:4]
    out_tiles = refs[4 : 4 + LINE]
    routes, slots, inverse, bits, depth, sems = refs[4 + LINE :]
    copies = start_all(
        [(routes_in, routes), (slots_in, slots), (inverse_in, inverse)] + in_parts(bits_in, bits, PARTS),
        sems,
    )
    depth[...] = jnp.zeros_like(depth)
    for copy in copies[:3]:
        copy.wait()
    for s in range(held):
        if s % (held // PARTS) == 0:
            copies[3 + s * PARTS // held].wait()
        weight = pixel_share(bits[s], inverse[s]).astype(jnp.bfloat16)
        depth[routes[s] * TILE_BLOCKS + slots[s]] += weight.astype(jnp.float32)
    for place, ref in enumerate(out_tiles):
        tile = tile_at(place)
        for b in range(TILE_BLOCKS):
            row, col = b // BLOCK_COLS * BLOCK, b % BLOCK_COLS * BLOCK
            ref[row : row + BLOCK, col : col + BLOCK] = depth[tile * TILE_BLOCKS + b].astype(
                jnp.bfloat16
            )


def edge_kernel(held, *refs):
    (
        routes_in, slots_in, kinds_in, inverse_in, coefs_in, bits_in, images_in, taps_in, col_taps_in, _,
        weighted, out_edge, _passed,
        routes, slots, kinds, inverse, coefs, bits, images, taps, col_taps, factors, total, sems,
    ) = refs
    strip = lax.axis_index("tile")
    copies = start_all(
        [
            (routes_in, routes), (slots_in, slots), (kinds_in, kinds), (inverse_in, inverse),
            (coefs_in, coefs), (taps_in, taps), (col_taps_in, col_taps),
        ]
        + in_parts(bits_in, bits, PARTS)
        + in_parts(images_in, images, PARTS),
        sems,
    )
    total[...] = jnp.zeros_like(total)
    for copy in copies[:6]:
        copy.wait()
    scales = tap_scales()
    for s in range(held):
        if s % (held // PARTS) == 0:
            copies[7 + s * PARTS // held].wait()
            copies[7 + PARTS + s * PARTS // held].wait()
        share = pixel_share(bits[s], inverse[s])
        pixels = (share * images[s].astype(jnp.float32)).astype(jnp.bfloat16)
        weighted[s] = pixels
        moved = jnp.dot(
            taps[1 - strip],
            jnp.concatenate([pixels, pixels], axis=0),
            preferred_element_type=jnp.float32,
        )
        crosses = (slots[s] // BLOCK_COLS == 1 - strip).astype(jnp.float32)
        factors[s * EDGE : (s + 1) * EDGE] = split_rows(
            moved, [crosses * coefs[k, kinds[s]] * float(1.0 / scales[k]) for k in range(3)]
        )
    copies[6].wait()
    result = jnp.dot(factors[...], col_taps[...], preferred_element_type=jnp.float32)
    for s in range(held):
        column = 1 + routes[s] * BLOCK_COLS + slots[s] % BLOCK_COLS
        spread_columns(total, column, pl.ds(0, EDGE), result[s * EDGE : (s + 1) * EDGE])
    for place in range(LINE):
        for b in range(BLOCK_COLS):
            out_edge[place, :, b * BLOCK : (b + 1) * BLOCK] = total[
                1 + tile_at(place) * BLOCK_COLS + b
            ].astype(jnp.bfloat16)


def match_kernel(held, ends, *refs):
    pl.when(at_end() == ends)(functools.partial(match_tiles, held, *refs))


def match_tiles(held, *refs):
    routes, slots, kinds, coefs, weighted, taps, col_taps = refs[:7]
    out_tiles = refs[-1 - LINE : -1]
    total = refs[-1]
    total[...] = jnp.zeros_like(total)
    scales = tap_scales()
    for first in range(0, held, 2):
        both = jnp.concatenate([weighted[first], weighted[first + 1]], axis=1)
        moved = jnp.dot(
            taps[...], jnp.concatenate([both, both], axis=0), preferred_element_type=jnp.float32
        )
        for n in range(2):
            s = first + n
            slot = slots[s]
            factors = split_rows(
                moved[:, n * BLOCK : (n + 1) * BLOCK],
                [coefs[k, kinds[s]] * float(1.0 / scales[k]) for k in range(3)],
            )
            result = jnp.dot(factors, col_taps[...], preferred_element_type=jnp.float32)
            row = pl.multiple_of(slot // BLOCK_COLS * BLOCK, 8)
            column = 1 + routes[s] * BLOCK_COLS + slot % BLOCK_COLS
            spread_columns(total, column, pl.ds(row, BLOCK + 2 * REACH), result)
    for place in range(LINE):
        for b in range(BLOCK_COLS):
            out_tiles[place][:, b * BLOCK : (b + 1) * BLOCK] = total[
                1 + tile_at(place) * BLOCK_COLS + b, pl.ds(REACH, TILE_ROWS)
            ]


def edge_rows():
    return pl.ds(pl.multiple_of((1 - lax.axis_index("tile")) * (TILE_ROWS - EDGE), EDGE), EDGE)


def relay_kernel(own, got, edge, _after, _, out, _passed):
    rows = edge_rows()
    out[...] = code(own[...] + decode(got[...]))
    out[rows] = code(own[rows] + edge[...].astype(jnp.float32) + decode(got[rows]))


def plus_kernel(own, got, *refs):
    out = refs[-2]
    out[...] = (own[...].astype(jnp.float32) + got[...].astype(jnp.float32)).astype(jnp.bfloat16)


def at_end():
    me = lax.axis_index("exp")
    return jnp.logical_or(me == 0, me == LINE - 1)


def turn_kernel(third, last, got, _, out, _passed):
    @pl.when(at_end())
    def _():
        out[...] = third[...]

    @pl.when(jnp.logical_not(at_end()))
    def _():
        out[...] = (last[...].astype(jnp.float32) + got[...].astype(jnp.float32)).astype(jnp.bfloat16)


def gather_kernel(
    third_d, last_d, got_d, got_mid_d, third_m, last_m, edge, got_m, out_sum, out_depth, out_inverse
):
    end = at_end()
    rows = edge_rows()
    out_sum[...] = jnp.where(end, last_m[...], third_m[...] + decode(got_m[...]))
    out_sum[rows] += jnp.where(end, edge[3].astype(jnp.float32), edge[2].astype(jnp.float32))
    own_d = jnp.where(end, last_d[...].astype(jnp.float32), third_d[...].astype(jnp.float32))
    denominator = (1.0 + own_d) + got_d[...].astype(jnp.float32) + got_mid_d[...].astype(jnp.float32)
    out_depth[...] = denominator
    out_inverse[...] = 1.0 / denominator


def coadded(matched, inverse, got_mid_m, got_last_m):
    return (matched[...] + decode(jnp.where(at_end(), got_last_m[...], got_mid_m[...]))) * inverse[...]


def term_kernel(matched, depth, inverse, got_mid_m, got_last_m, out_term):
    coadd = coadded(matched, inverse, got_mid_m, got_last_m)
    out_term[...] = (coadd * coadd * depth[...]).astype(jnp.bfloat16)


def coadd_kernel(matched, inverse, got_mid_m, got_last_m, out_coadd):
    out_coadd[...] = coadded(matched, inverse, got_mid_m, got_last_m)


def first_kernel(tile_0, tile_1, tile_2, edge, far, next_far, third):
    rows = edge_rows()
    for place, (source, out) in enumerate(((tile_0, far), (tile_1, next_far), (tile_2, third))):
        out[...] = code(source[...])
        out[rows] = code(source[rows] + edge[place].astype(jnp.float32))


def in_vmem(count):
    return [pl.BlockSpec(memory_space=pltpu.VMEM)] * count


def in_smem(count):
    return [pl.BlockSpec(memory_space=pltpu.SMEM)] * count


def in_hbm(count):
    return [pl.BlockSpec(memory_space=pltpu.HBM)] * count


def vmem_limit(mebibytes):
    return pltpu.CompilerParams(vmem_limit_bytes=mebibytes * MEBI)


def work(microseconds):
    return pl.CostEstimate(
        flops=microseconds * 1_150_000_000, bytes_accessed=0, transcendentals=0
    )


def reduced(images, mask_bits, inv_var, routes, block_slot, kernel_index, coefficients):
    held = images.shape[2]
    tile = jax.ShapeDtypeStruct((TILE_ROWS, TILE_COLS), jnp.bfloat16)
    wide = jax.ShapeDtypeStruct((TILE_ROWS, TILE_COLS), jnp.float32)
    columns = LINE * BLOCK_COLS + 2
    target, slot, kind = routes.reshape(held), block_slot.reshape(held), kernel_index.reshape(held)
    mixing = coefficients.T
    in_place = [pl.BlockSpec(memory_space=pl.ANY)]
    beside = [(0, 1), (1, 0), (2, 3), (3, 2)]
    across = [(1, 2), (2, 1)]

    scalars = [pltpu.SMEM((held,), kind) for kind in (jnp.int32, jnp.int32, jnp.float32)]
    blocks = jax.ShapeDtypeStruct((held, BLOCK, BLOCK), jnp.bfloat16)
    far_d, next_d, third_d, last_d = pl.pallas_call(
        functools.partial(depth_kernel, held),
        out_shape=[tile] * LINE,
        in_specs=in_hbm(4),
        out_specs=in_vmem(LINE),
        scratch_shapes=scalars
        + [
            pltpu.VMEM((held, BLOCK, BLOCK), jnp.int32),
            pltpu.VMEM((LINE * TILE_BLOCKS, BLOCK, BLOCK), jnp.float32),
            pltpu.SemaphoreType.DMA((3 + PARTS,)),
        ],
        compiler_params=vmem_limit(56),
        cost_estimate=work(2),
        name="depth",
    )(target, slot, inv_var.reshape(held), mask_bits[0, 0])
    got_far_d = lax.ppermute(far_d, "exp", [(0, 1), (LINE - 1, LINE - 2)])

    edge_taps = np.stack([row_taps(np.arange(-EDGE, 0)), row_taps(np.arange(BLOCK, BLOCK + EDGE))])
    col_taps = jnp.asarray(column_taps())
    weighted, edge, next_d = pl.pallas_call(
        functools.partial(edge_kernel, held),
        out_shape=[blocks, jax.ShapeDtypeStruct((LINE, EDGE, TILE_COLS), jnp.bfloat16), tile],
        in_specs=in_hbm(9) + in_place,
        out_specs=in_vmem(2) + in_place,
        input_output_aliases={9: 2},
        scratch_shapes=[pltpu.SMEM((held,), jnp.int32)]
        + scalars
        + [
            pltpu.SMEM(mixing.shape, jnp.float32),
            pltpu.VMEM((held, BLOCK, BLOCK), jnp.int32),
            pltpu.VMEM((held, BLOCK, BLOCK), jnp.bfloat16),
            pltpu.VMEM(edge_taps.shape, jnp.bfloat16),
            pltpu.VMEM(col_taps.shape, jnp.bfloat16),
            pltpu.VMEM((held * EDGE, 6 * BLOCK), jnp.bfloat16),
            pltpu.VMEM((columns, EDGE, BLOCK), jnp.float32),
            pltpu.SemaphoreType.DMA((7 + 2 * PARTS,)),
        ],
        compiler_params=vmem_limit(24),
        cost_estimate=work(3),
        name="edges",
    )(
        target, slot, kind, inv_var.reshape(held), mixing, mask_bits[0, 0], images[0, 0],
        jnp.asarray(edge_taps), col_taps, next_d,
    )
    other_edge = lax.ppermute(edge, "tile", [(0, 1), (1, 0)])
    got_next_d = lax.ppermute(next_d, "exp", [(0, 1), (LINE - 1, LINE - 2)])
    own_rows = jnp.asarray(row_taps(np.arange(-REACH, BLOCK + REACH)))

    def match(ends, after):
        return pl.pallas_call(
            functools.partial(match_kernel, held, ends),
            out_shape=[wide] * LINE,
            in_specs=in_smem(4) + in_vmem(3) + in_place * len(after),
            out_specs=in_vmem(LINE),
            scratch_shapes=[pltpu.VMEM((columns, TILE_ROWS + 2 * REACH, BLOCK), jnp.float32)],
            compiler_params=vmem_limit(24),
            cost_estimate=work(0),
            name="match",
        )(target, slot, kind, mixing, weighted, own_rows, col_taps, *after)

    end_tiles = match(True, [])
    far_m, next_m, third_m = pl.pallas_call(
        first_kernel,
        out_shape=[tile, tile, tile],
        in_specs=in_vmem(4),
        out_specs=in_vmem(3),
        compiler_params=vmem_limit(24),
        cost_estimate=work(0),
        name="first",
    )(*end_tiles[:3], other_edge)

    def passing(kernel, name, operands, after, passed):
        return pl.pallas_call(
            kernel,
            out_shape=[tile, jax.ShapeDtypeStruct(passed.shape, passed.dtype)],
            in_specs=in_vmem(len(operands)) + in_place * (len(after) + 1),
            out_specs=in_vmem(1) + in_place,
            input_output_aliases={len(operands) + len(after): 1},
            compiler_params=vmem_limit(24),
            cost_estimate=work(1),
            name=name,
        )(*operands, *after, passed)

    got_far_m = lax.ppermute(far_m, "exp", [(0, 1), (LINE - 1, LINE - 2)])
    far_sum, next_m = passing(plus_kernel, "plus", [far_d, got_far_d], [], next_m)
    mid_far_d = lax.ppermute(far_sum, "exp", across)
    mid_tiles = match(False, [far_sum])
    next_sum, next_m = passing(plus_kernel, "plus", [next_d, got_next_d], [mid_tiles[0]], next_m)
    got_next_m = lax.ppermute(next_m, "exp", beside)
    mid_d = lax.ppermute(next_sum, "exp", across)
    far_relayed, third_m = passing(
        relay_kernel, "relay", [mid_tiles[0], got_far_m, other_edge[0]], [mid_far_d], third_m
    )
    mid_far_m = lax.ppermute(far_relayed, "exp", across)
    turned, third_m = passing(turn_kernel, "turn", [third_d, last_d, mid_far_d], [], third_m)
    got_d = lax.ppermute(turned, "exp", beside)
    next_relayed, third_m = passing(
        relay_kernel, "relay", [mid_tiles[1], got_next_m, other_edge[1]], [mid_d], third_m
    )
    mid_m = lax.ppermute(next_relayed, "exp", across)
    got_m = lax.ppermute(third_m, "exp", [(0, 1), (LINE - 1, LINE - 2)])
    last_relayed, _ = passing(
        relay_kernel, "relay", [mid_tiles[3], mid_far_m, other_edge[3]], [got_d], jnp.zeros((8, 128), jnp.float32)
    )
    end_m = lax.ppermute(last_relayed, "exp", [(1, 0), (LINE - 2, LINE - 1)])
    matched, depth, inverse = pl.pallas_call(
        gather_kernel,
        out_shape=[wide] * 3,
        in_specs=in_vmem(8),
        out_specs=in_vmem(3),
        compiler_params=vmem_limit(24),
        cost_estimate=work(1),
        name="gather",
    )(third_d, last_d, got_d, mid_d, mid_tiles[2], end_tiles[3], other_edge, got_m)

    def ending(kernel, name, shape, *operands):
        return pl.pallas_call(
            kernel,
            out_shape=shape,
            in_specs=in_vmem(len(operands)),
            out_specs=pl.BlockSpec(memory_space=pltpu.VMEM),
            compiler_params=vmem_limit(24),
            cost_estimate=work(1),
            name=name,
        )(*operands)

    term = ending(term_kernel, "term", tile, matched, depth, inverse, mid_m, end_m)
    coadd = ending(coadd_kernel, "coadd", wide, matched, inverse, mid_m, end_m)
    other_term = lax.ppermute(term, "band", [(0, 1), (1, 0)])
    detection = term.astype(jnp.float32) + other_term.astype(jnp.float32)
    return (coadd[None], detection)


def local(images, mask_bits, inv_var, routes, block_slot, kernel_index, coefficients):
    peers = lax.axis_size("exp")
    partial_sums_fit = peers * TILE_BLOCKS <= 2 * images.shape[2]
    pairs = lax.axis_size("tile") == 2 and lax.axis_size("band") == 2
    plan = reduced if partial_sums_fit and pairs and peers == LINE else routed
    return plan(images, mask_bits, inv_var, routes, block_slot, kernel_index, coefficients)


def solution(mesh):
    return jax.shard_map(
        local,
        mesh=mesh,
        in_specs=(
            P(("patch", "band"), "tile", "exp", None, None),
            P(("patch", "band"), "tile", "exp", None, None),
            P(("patch", "band"), "tile", "exp"),
            P(("patch", "band"), "tile", "exp", None),
            P(("patch", "band"), "tile", "exp"),
            P(("patch", "band"), "tile", "exp"),
            P(),
        ),
        out_specs=(P(("patch", "band"), "tile", "exp"), P(("patch", "tile"), "exp")),
        check_vma=False,
    )
```

```python
import functools

import jax
import jax.numpy as jnp
import ml_dtypes
import numpy as np
from jax import lax
from jax.experimental import pallas as pl
from jax.experimental.pallas import tpu as pltpu
from jax.sharding import PartitionSpec as P

BLOCK = 128
TAPS = 41
BLOCK_ROWS = 2
BLOCK_COLS = 4


kernel_sigmas = (1.0, 2.5, 6.0)


def extended(block, sides, width):
    for axis, dim in sides:
        count = lax.axis_size(axis)
        forward = [(i, i + 1) for i in range(count - 1)]
        backward = [(target, source) for source, target in forward]
        low = lax.ppermute(
            lax.slice_in_dim(block, block.shape[dim] - width, None, axis=dim), axis, forward
        )
        high = lax.ppermute(lax.slice_in_dim(block, 0, width, axis=dim), axis, backward)
        block = jnp.concatenate([low, block, high], axis=dim)
    return block


def usable_share(bits):
    flagged = jnp.bitwise_and(bits, 6) == 6
    suspect = jnp.bitwise_and(bits, 1).astype(jnp.float32)
    return jnp.where(flagged, 0.0, 1.0 - 0.5 * suspect)


def band_matrix(length, half_span):
    rows_here = jnp.arange(length + 2 * half_span, dtype=jnp.int32)[:, None]
    cols_here = jnp.arange(length, dtype=jnp.int32)[None, :]
    offset = (rows_here - cols_here - half_span).astype(jnp.float32)
    inside = jnp.abs(offset) <= half_span
    taps_axis = jnp.arange(-half_span, half_span + 1).astype(jnp.float32)
    result = []
    for spread in kernel_sigmas:
        norm_sum = jnp.sum(jnp.exp(-taps_axis * taps_axis / (2.0 * spread * spread)))
        result.append(
            jnp.where(inside, jnp.exp(-offset * offset / (2.0 * spread * spread)), 0.0) / norm_sum
        )
    return jnp.stack(result)


def routed(images, mask_bits, inv_var, routes, block_slot, kernel_index, coefficients):
    peer_count = lax.axis_size("exp")
    held_count = images.shape[2]
    capacity = max(2, 2 * held_count // peer_count)
    slot_count = peer_count * capacity
    pixels = BLOCK * BLOCK
    tile_blocks = BLOCK_ROWS * BLOCK_COLS
    coef_count = coefficients.shape[0]
    usable = usable_share(mask_bits[0, 0])
    inverse = inv_var[0, 0][:, None, None]
    weight = (usable * inverse).astype(jnp.bfloat16).reshape(held_count, pixels)
    weighted = (
        (usable * inverse * images[0, 0].astype(jnp.float32))
        .astype(jnp.bfloat16)
        .reshape(held_count, pixels)
    )
    target = routes[0, 0, :, 0]
    ordinal = jnp.arange(held_count, dtype=jnp.int32)
    same_target = target[:, None] == target[None, :]
    earlier = jnp.sum(
        (same_target & (ordinal[None, :] < ordinal[:, None])).astype(jnp.int32), axis=1
    )
    position = target * capacity + earlier
    placed = jnp.arange(slot_count, dtype=jnp.int32)[:, None] == position[None, :]
    placed_int = placed.astype(jnp.int32)
    slot_block = jnp.sum(placed_int * (block_slot[0, 0] + 1)[None, :], axis=1) - 1
    slot_kernel = jnp.sum(placed_int * kernel_index[0, 0][None, :], axis=1)
    labels = jnp.stack([slot_block, slot_kernel], axis=1).reshape(peer_count, capacity, 2)
    placed_half = placed.astype(jnp.bfloat16)
    send_weight = (
        jnp.dot(placed_half, weight, preferred_element_type=jnp.float32)
        .astype(jnp.bfloat16)
        .reshape(peer_count, capacity, pixels)
    )
    block_ids = jnp.arange(tile_blocks, dtype=jnp.int32)[:, None]
    send_weighted = (
        jnp.dot(placed_half, weighted, preferred_element_type=jnp.float32)
        .astype(jnp.bfloat16)
        .reshape(peer_count, capacity, pixels)
    )
    got_weighted, got_weight, got_labels = (
        lax.all_to_all(send_weighted, "exp", split_axis=0, concat_axis=0, tiled=True),
        lax.all_to_all(send_weight, "exp", split_axis=0, concat_axis=0, tiled=True),
        lax.all_to_all(labels, "exp", split_axis=0, concat_axis=0, tiled=True),
    )
    got_labels = got_labels.reshape(slot_count, 2)
    into_block = block_ids == got_labels[:, 0][None, :]
    kernel_pick = (
        got_labels[:, 1][:, None] == jnp.arange(coef_count, dtype=jnp.int32)[None, :]
    ).astype(jnp.float32)
    slot_mix = jnp.dot(kernel_pick, coefficients, precision=lax.Precision.HIGHEST)
    mixing = slot_mix.T[:, None, :] * into_block.astype(jnp.float32)[None, :, :]
    basis_sum = jnp.einsum(
        "kbp,px->kbx",
        mixing,
        got_weighted.reshape(slot_count, pixels).astype(jnp.float32),
        precision=lax.Precision.HIGHEST,
    )
    depth_sum = jnp.dot(
        into_block.astype(jnp.bfloat16),
        got_weight.reshape(slot_count, pixels),
        preferred_element_type=jnp.float32,
    )
    tile_rows = BLOCK_ROWS * BLOCK
    tile_cols = BLOCK_COLS * BLOCK
    basis_tile = (
        basis_sum.reshape(3, BLOCK_ROWS, BLOCK_COLS, BLOCK, BLOCK)
        .transpose(0, 1, 3, 2, 4)
        .reshape(3, tile_rows, tile_cols)
    )
    depth_tile = (
        depth_sum.reshape(BLOCK_ROWS, BLOCK_COLS, BLOCK, BLOCK)
        .transpose(0, 2, 1, 3)
        .reshape(tile_rows, tile_cols)
    )
    half_span = TAPS // 2
    column_mix = band_matrix(tile_cols, half_span)
    row_mix = band_matrix(tile_rows, half_span).transpose(0, 2, 1)
    framed = extended(basis_tile, (("exp", 2), ("tile", 1)), half_span)
    across = jnp.einsum("kyp,kpc->kyc", framed, column_mix, precision=lax.Precision.HIGHEST)
    matched = jnp.einsum("kry,kyc->rc", row_mix, across, precision=lax.Precision.HIGHEST)
    denominator = 1.0 + depth_tile
    coadded = matched / denominator
    detection = lax.psum(coadded * coadded * denominator, "band")
    return (coadded[None], detection)


HALF = TAPS // 2
EDGE = 32
REACH = 24
LINE = 4
PARTS = 4
TILE_BLOCKS = BLOCK_ROWS * BLOCK_COLS
TILE_ROWS = BLOCK_ROWS * BLOCK
TILE_COLS = BLOCK_COLS * BLOCK
MEBI = 1024 * 1024


def tap_values(offset):
    span = np.arange(-HALF, HALF + 1, dtype=np.float64)
    inside = np.abs(offset) <= HALF
    result = []
    for spread in kernel_sigmas:
        total = np.exp(-span * span / (2.0 * spread * spread)).sum()
        value = np.exp(-offset.astype(np.float64) ** 2 / (2.0 * spread * spread)) / total
        result.append(np.where(inside, value, 0.0))
    return np.stack(result)


def split_taps(values):
    high = values.astype(ml_dtypes.bfloat16)
    low = (values - high.astype(np.float64)).astype(ml_dtypes.bfloat16)
    return high, low


def row_taps(target):
    values = tap_values(target[:, None] - np.arange(BLOCK)[None, :])
    return np.concatenate(split_taps(values.reshape(-1, BLOCK)), axis=1)


def tap_scales():
    values = tap_values(np.arange(-HALF, HALF + 1))[:, None, :]
    factors = np.linspace(1.0, 2.0, 4096, endpoint=False)[None, :, None]
    rounded = (values * factors).astype(ml_dtypes.bfloat16).astype(np.float64) / factors
    return factors[0, np.argmin(((rounded - values) ** 2).sum(axis=-1), axis=1), 0]


def column_taps():
    lane = np.arange(BLOCK)
    beside = np.where(lane < BLOCK // 2, lane + BLOCK, lane - BLOCK)
    target = np.concatenate([lane, beside])[None, :]
    values = tap_values(target - lane[:, None]) * tap_scales()[:, None, None]
    rounded = values.reshape(3 * BLOCK, 2 * BLOCK).astype(ml_dtypes.bfloat16)
    return np.concatenate([rounded, rounded], axis=0)


def code(value):
    return (value * jnp.abs(value)).astype(jnp.bfloat16)


def decode(coded):
    square = coded.astype(jnp.float32)
    root = jnp.sqrt(jnp.abs(square))
    return jnp.where(square < 0, -root, root)


def tile_at(place):
    me = lax.axis_index("exp")
    return jnp.where(me < LINE // 2, LINE - 1 - place, place)


def split_rows(block, mixing):
    rows = block.shape[0] // 3
    high, low = [], []
    for k in range(3):
        value = mixing[k] * block[k * rows : (k + 1) * rows]
        rounded = value.astype(jnp.bfloat16)
        high.append(rounded)
        low.append((value - rounded.astype(jnp.float32)).astype(jnp.bfloat16))
    return jnp.concatenate(high + low, axis=1)


def spread_columns(target, column, rows, values):
    beside = values[:, BLOCK:]
    to_right = lax.broadcasted_iota(jnp.int32, beside.shape, 1) < BLOCK // 2
    target[column, rows] += values[:, :BLOCK]
    target[column + 1, rows] += jnp.where(to_right, beside, 0.0)
    target[column - 1, rows] += jnp.where(to_right, 0.0, beside)


def pixel_share(flags, full):
    part = jnp.where((flags & 1) == 1, 0.5 * full, full)
    return jnp.where((flags & 6) == 6, 0.0, part)


def start_all(pairs, sems):
    copies = [pltpu.make_async_copy(src, dst, sems.at[n]) for n, (src, dst) in enumerate(pairs)]
    for copy in copies:
        copy.start()
    return copies


def in_parts(src, dst, parts):
    size = src.shape[0] // parts
    return [(src.at[pl.ds(p * size, size)], dst.at[pl.ds(p * size, size)]) for p in range(parts)]


def depth_kernel(held, *refs):
    routes_in, slots_in, inverse_in, bits_in = refs[:4]
    out_tiles = refs[4 : 4 + LINE]
    routes, slots, inverse, bits, depth, sems = refs[4 + LINE :]
    copies = start_all(
        [(routes_in, routes), (slots_in, slots), (inverse_in, inverse)] + in_parts(bits_in, bits, PARTS),
        sems,
    )
    depth[...] = jnp.zeros_like(depth)
    for copy in copies[:3]:
        copy.wait()
    for s in range(held):
        if s % (held // PARTS) == 0:
            copies[3 + s * PARTS // held].wait()
        weight = pixel_share(bits[s], inverse[s]).astype(jnp.bfloat16)
        depth[routes[s] * TILE_BLOCKS + slots[s]] += weight.astype(jnp.float32)
    for place, ref in enumerate(out_tiles):
        tile = tile_at(place)
        for b in range(TILE_BLOCKS):
            row, col = b // BLOCK_COLS * BLOCK, b % BLOCK_COLS * BLOCK
            ref[row : row + BLOCK, col : col + BLOCK] = depth[tile * TILE_BLOCKS + b].astype(
                jnp.bfloat16
            )


def edge_kernel(held, *refs):
    (
        routes_in, slots_in, kinds_in, inverse_in, coefs_in, bits_in, images_in, taps_in, col_taps_in, passed_in,
        weighted, out_edge, passed,
        routes, slots, kinds, inverse, coefs, bits, images, taps, col_taps, factors, total, sems,
    ) = refs
    strip = lax.axis_index("tile")
    copies = start_all(
        [
            (routes_in, routes), (slots_in, slots), (kinds_in, kinds), (inverse_in, inverse),
            (coefs_in, coefs), (taps_in, taps), (col_taps_in, col_taps),
        ]
        + in_parts(bits_in, bits, PARTS)
        + in_parts(images_in, images, PARTS)
        + [(passed_in, passed)],
        sems,
    )
    total[...] = jnp.zeros_like(total)
    for copy in copies[:6]:
        copy.wait()
    scales = tap_scales()
    for s in range(held):
        if s % (held // PARTS) == 0:
            copies[7 + s * PARTS // held].wait()
            copies[7 + PARTS + s * PARTS // held].wait()
        share = pixel_share(bits[s], inverse[s])
        pixels = (share * images[s].astype(jnp.float32)).astype(jnp.bfloat16)
        weighted[s] = pixels
        moved = jnp.dot(
            taps[1 - strip],
            jnp.concatenate([pixels, pixels], axis=0),
            preferred_element_type=jnp.float32,
        )
        crosses = (slots[s] // BLOCK_COLS == 1 - strip).astype(jnp.float32)
        factors[s * EDGE : (s + 1) * EDGE] = split_rows(
            moved, [crosses * coefs[k, kinds[s]] * float(1.0 / scales[k]) for k in range(3)]
        )
    copies[6].wait()
    copies[-1].wait()
    result = jnp.dot(factors[...], col_taps[...], preferred_element_type=jnp.float32)
    for s in range(held):
        column = 1 + routes[s] * BLOCK_COLS + slots[s] % BLOCK_COLS
        spread_columns(total, column, pl.ds(0, EDGE), result[s * EDGE : (s + 1) * EDGE])
    for place in range(LINE):
        for b in range(BLOCK_COLS):
            out_edge[place, :, b * BLOCK : (b + 1) * BLOCK] = total[
                1 + tile_at(place) * BLOCK_COLS + b
            ].astype(jnp.bfloat16)


def match_kernel(held, ends, *refs):
    pl.when(at_end() == ends)(functools.partial(match_tiles, held, *refs))


def match_tiles(held, *refs):
    routes, slots, kinds, coefs, weighted, taps, col_taps = refs[:7]
    out_tiles = refs[-1 - LINE : -1]
    total = refs[-1]
    total[...] = jnp.zeros_like(total)
    scales = tap_scales()
    for first in range(0, held, 2):
        both = jnp.concatenate([weighted[first], weighted[first + 1]], axis=1)
        moved = jnp.dot(
            taps[...], jnp.concatenate([both, both], axis=0), preferred_element_type=jnp.float32
        )
        for n in range(2):
            s = first + n
            slot = slots[s]
            factors = split_rows(
                moved[:, n * BLOCK : (n + 1) * BLOCK],
                [coefs[k, kinds[s]] * float(1.0 / scales[k]) for k in range(3)],
            )
            result = jnp.dot(factors, col_taps[...], preferred_element_type=jnp.float32)
            row = pl.multiple_of(slot // BLOCK_COLS * BLOCK, 8)
            column = 1 + routes[s] * BLOCK_COLS + slot % BLOCK_COLS
            spread_columns(total, column, pl.ds(row, BLOCK + 2 * REACH), result)
    for place in range(LINE):
        for b in range(BLOCK_COLS):
            out_tiles[place][:, b * BLOCK : (b + 1) * BLOCK] = total[
                1 + tile_at(place) * BLOCK_COLS + b, pl.ds(REACH, TILE_ROWS)
            ]


def edge_rows():
    return pl.ds(pl.multiple_of((1 - lax.axis_index("tile")) * (TILE_ROWS - EDGE), EDGE), EDGE)


def relay_kernel(own, got, edge, *refs):
    out = refs[-2]
    rows = edge_rows()
    out[...] = code(own[...] + decode(got[...]))
    out[rows] = code(own[rows] + edge[...].astype(jnp.float32) + decode(got[rows]))


def plus_kernel(own, got, *refs):
    out = refs[-2]
    out[...] = (own[...].astype(jnp.float32) + got[...].astype(jnp.float32)).astype(jnp.bfloat16)


def add_copy_kernel(own, got, share, _after, out, share_out):
    out[...] = (own[...].astype(jnp.float32) + got[...].astype(jnp.float32)).astype(jnp.bfloat16)
    share_out[...] = share[...]


def at_end():
    me = lax.axis_index("exp")
    return jnp.logical_or(me == 0, me == LINE - 1)


def turn_kernel(third, last, got, _, out, _passed):
    @pl.when(at_end())
    def _():
        out[...] = third[...]

    @pl.when(jnp.logical_not(at_end()))
    def _():
        out[...] = (last[...].astype(jnp.float32) + got[...].astype(jnp.float32)).astype(jnp.bfloat16)


def gather_kernel(
    third_d, last_d, got_d, got_mid_d, third_m, last_m, edge, got_m, out_sum, out_depth, out_inverse
):
    end = at_end()
    rows = edge_rows()
    out_sum[...] = jnp.where(end, last_m[...], third_m[...] + decode(got_m[...]))
    out_sum[rows] += jnp.where(end, edge[3].astype(jnp.float32), edge[2].astype(jnp.float32))
    own_d = jnp.where(end, last_d[...].astype(jnp.float32), third_d[...].astype(jnp.float32))
    denominator = (1.0 + own_d) + got_d[...].astype(jnp.float32) + got_mid_d[...].astype(jnp.float32)
    out_depth[...] = denominator
    out_inverse[...] = 1.0 / denominator


def coadded(matched, inverse, got_mid_m, got_last_m):
    return (matched[...] + decode(jnp.where(at_end(), got_last_m[...], got_mid_m[...]))) * inverse[...]


def term_kernel(matched, depth, inverse, got_mid_m, got_last_m, out_term):
    coadd = coadded(matched, inverse, got_mid_m, got_last_m)
    out_term[...] = (coadd * coadd * depth[...]).astype(jnp.bfloat16)


def coadd_kernel(matched, inverse, got_mid_m, got_last_m, out_coadd):
    out_coadd[...] = coadded(matched, inverse, got_mid_m, got_last_m)


def first_kernel(tile_0, tile_1, tile_2, edge, far, next_far, third):
    rows = edge_rows()
    for place, (source, out) in enumerate(((tile_0, far), (tile_1, next_far), (tile_2, third))):
        out[...] = code(source[...])
        out[rows] = code(source[rows] + edge[place].astype(jnp.float32))


def in_vmem(count):
    return [pl.BlockSpec(memory_space=pltpu.VMEM)] * count


def in_smem(count):
    return [pl.BlockSpec(memory_space=pltpu.SMEM)] * count


def in_hbm(count):
    return [pl.BlockSpec(memory_space=pltpu.HBM)] * count


def vmem_limit(mebibytes):
    return pltpu.CompilerParams(vmem_limit_bytes=mebibytes * MEBI)


def work(microseconds):
    return pl.CostEstimate(
        flops=microseconds * 1_150_000_000, bytes_accessed=0, transcendentals=0
    )


def reduced(images, mask_bits, inv_var, routes, block_slot, kernel_index, coefficients):
    held = images.shape[2]
    tile = jax.ShapeDtypeStruct((TILE_ROWS, TILE_COLS), jnp.bfloat16)
    wide = jax.ShapeDtypeStruct((TILE_ROWS, TILE_COLS), jnp.float32)
    columns = LINE * BLOCK_COLS + 2
    target, slot, kind = routes.reshape(held), block_slot.reshape(held), kernel_index.reshape(held)
    mixing = coefficients.T
    in_place = [pl.BlockSpec(memory_space=pl.ANY)]
    beside = [(0, 1), (1, 0), (2, 3), (3, 2)]
    across = [(1, 2), (2, 1)]

    scalars = [pltpu.SMEM((held,), kind) for kind in (jnp.int32, jnp.int32, jnp.float32)]
    blocks = jax.ShapeDtypeStruct((held, BLOCK, BLOCK), jnp.bfloat16)
    far_d, next_d, third_d, last_d = pl.pallas_call(
        functools.partial(depth_kernel, held),
        out_shape=[tile] * LINE,
        in_specs=in_hbm(4),
        out_specs=in_vmem(LINE),
        scratch_shapes=scalars
        + [
            pltpu.VMEM((held, BLOCK, BLOCK), jnp.int32),
            pltpu.VMEM((LINE * TILE_BLOCKS, BLOCK, BLOCK), jnp.float32),
            pltpu.SemaphoreType.DMA((3 + PARTS,)),
        ],
        compiler_params=vmem_limit(56),
        cost_estimate=work(2),
        name="depth",
    )(target, slot, inv_var.reshape(held), mask_bits[0, 0])
    got_far_d = lax.ppermute(far_d, "exp", [(0, 1), (LINE - 1, LINE - 2)])

    edge_taps = np.stack([row_taps(np.arange(-EDGE, 0)), row_taps(np.arange(BLOCK, BLOCK + EDGE))])
    col_taps = jnp.asarray(column_taps())
    weighted, edge, next_d = pl.pallas_call(
        functools.partial(edge_kernel, held),
        out_shape=[blocks, jax.ShapeDtypeStruct((LINE, EDGE, TILE_COLS), jnp.bfloat16), tile],
        in_specs=in_hbm(10),
        out_specs=in_vmem(3),
        scratch_shapes=[pltpu.SMEM((held,), jnp.int32)]
        + scalars
        + [
            pltpu.SMEM(mixing.shape, jnp.float32),
            pltpu.VMEM((held, BLOCK, BLOCK), jnp.int32),
            pltpu.VMEM((held, BLOCK, BLOCK), jnp.bfloat16),
            pltpu.VMEM(edge_taps.shape, jnp.bfloat16),
            pltpu.VMEM(col_taps.shape, jnp.bfloat16),
            pltpu.VMEM((held * EDGE, 6 * BLOCK), jnp.bfloat16),
            pltpu.VMEM((columns, EDGE, BLOCK), jnp.float32),
            pltpu.SemaphoreType.DMA((8 + 2 * PARTS,)),
        ],
        compiler_params=vmem_limit(24),
        cost_estimate=work(3),
        name="edges",
    )(
        target, slot, kind, inv_var.reshape(held), mixing, mask_bits[0, 0], images[0, 0],
        jnp.asarray(edge_taps), col_taps, next_d,
    )
    other_edge = lax.ppermute(edge, "tile", [(0, 1), (1, 0)])
    got_next_d = lax.ppermute(next_d, "exp", [(0, 1), (LINE - 1, LINE - 2)])
    own_rows = jnp.asarray(row_taps(np.arange(-REACH, BLOCK + REACH)))

    def match(ends, after):
        return pl.pallas_call(
            functools.partial(match_kernel, held, ends),
            out_shape=[wide] * LINE,
            in_specs=in_smem(4) + in_vmem(3) + in_place * len(after),
            out_specs=in_vmem(LINE),
            scratch_shapes=[pltpu.VMEM((columns, TILE_ROWS + 2 * REACH, BLOCK), jnp.float32)],
            compiler_params=vmem_limit(24),
            cost_estimate=work(0),
            name="match",
        )(target, slot, kind, mixing, weighted, own_rows, col_taps, *after)

    end_tiles = match(True, [])
    far_m, next_m, third_m = pl.pallas_call(
        first_kernel,
        out_shape=[tile, tile, tile],
        in_specs=in_vmem(4),
        out_specs=in_vmem(3),
        compiler_params=vmem_limit(24),
        cost_estimate=work(0),
        name="first",
    )(*end_tiles[:3], other_edge)

    def passing(kernel, name, operands, after, passed):
        return pl.pallas_call(
            kernel,
            out_shape=[tile, jax.ShapeDtypeStruct(passed.shape, passed.dtype)],
            in_specs=in_vmem(len(operands)) + in_place * (len(after) + 1),
            out_specs=in_vmem(1) + in_place,
            input_output_aliases={len(operands) + len(after): 1},
            compiler_params=vmem_limit(24),
            cost_estimate=work(1),
            name=name,
        )(*operands, *after, passed)

    nothing = jnp.zeros((8, 128), jnp.float32)
    got_far_m = lax.ppermute(far_m, "exp", [(0, 1), (LINE - 1, LINE - 2)])
    far_sum, next_m = passing(plus_kernel, "plus", [far_d, got_far_d], [], next_m)
    mid_far_d = lax.ppermute(far_sum, "exp", across)
    mid_tiles = match(False, [far_sum])
    next_sum, next_m = pl.pallas_call(
        add_copy_kernel,
        out_shape=[tile, tile],
        in_specs=in_vmem(3) + in_place,
        out_specs=in_vmem(2),
        compiler_params=vmem_limit(24),
        cost_estimate=work(1),
        name="plus",
    )(next_d, got_next_d, next_m, mid_tiles[0])
    got_next_m = lax.ppermute(next_m, "exp", beside)
    mid_d = lax.ppermute(next_sum, "exp", across)
    far_relayed, third_m = passing(
        relay_kernel, "relay", [mid_tiles[0], got_far_m, other_edge[0]], [mid_far_d], third_m
    )
    mid_far_m = lax.ppermute(far_relayed, "exp", across)
    turned, _ = passing(turn_kernel, "turn", [third_d, last_d, mid_far_d], [], nothing)
    got_d = lax.ppermute(turned, "exp", beside)
    next_relayed, third_m = passing(
        relay_kernel, "relay", [mid_tiles[1], got_next_m, other_edge[1]], [], third_m
    )
    mid_m = lax.ppermute(next_relayed, "exp", across)
    got_m = lax.ppermute(third_m, "exp", [(0, 1), (LINE - 1, LINE - 2)])
    last_relayed, _ = passing(
        relay_kernel, "relay", [mid_tiles[3], mid_far_m, other_edge[3]], [got_d, mid_d], nothing
    )
    end_m = lax.ppermute(last_relayed, "exp", [(1, 0), (LINE - 2, LINE - 1)])
    matched, depth, inverse = pl.pallas_call(
        gather_kernel,
        out_shape=[wide] * 3,
        in_specs=in_vmem(8),
        out_specs=in_vmem(3),
        compiler_params=vmem_limit(24),
        cost_estimate=work(1),
        name="gather",
    )(third_d, last_d, got_d, mid_d, mid_tiles[2], end_tiles[3], other_edge, got_m)

    def ending(kernel, name, shape, *operands):
        return pl.pallas_call(
            kernel,
            out_shape=shape,
            in_specs=in_vmem(len(operands)),
            out_specs=pl.BlockSpec(memory_space=pltpu.VMEM),
            compiler_params=vmem_limit(24),
            cost_estimate=work(1),
            name=name,
        )(*operands)

    term = ending(term_kernel, "term", tile, matched, depth, inverse, mid_m, end_m)
    coadd = ending(coadd_kernel, "coadd", wide, matched, inverse, mid_m, end_m)
    other_term = lax.ppermute(term, "band", [(0, 1), (1, 0)])
    detection = term.astype(jnp.float32) + other_term.astype(jnp.float32)
    return (coadd[None], detection)


def local(images, mask_bits, inv_var, routes, block_slot, kernel_index, coefficients):
    peers = lax.axis_size("exp")
    partial_sums_fit = peers * TILE_BLOCKS <= 2 * images.shape[2]
    pairs = lax.axis_size("tile") == 2 and lax.axis_size("band") == 2
    plan = reduced if partial_sums_fit and pairs and peers == LINE else routed
    return plan(images, mask_bits, inv_var, routes, block_slot, kernel_index, coefficients)


def solution(mesh):
    return jax.shard_map(
        local,
        mesh=mesh,
        in_specs=(
            P(("patch", "band"), "tile", "exp", None, None),
            P(("patch", "band"), "tile", "exp", None, None),
            P(("patch", "band"), "tile", "exp"),
            P(("patch", "band"), "tile", "exp", None),
            P(("patch", "band"), "tile", "exp"),
            P(("patch", "band"), "tile", "exp"),
            P(),
        ),
        out_specs=(P(("patch", "band"), "tile", "exp"), P(("patch", "tile"), "exp")),
        check_vma=False,
    )
```

```python
import functools

import jax
import jax.numpy as jnp
import ml_dtypes
import numpy as np
from jax import lax
from jax.experimental import pallas as pl
from jax.experimental.pallas import tpu as pltpu
from jax.sharding import PartitionSpec as P

BLOCK = 128
TAPS = 41
BLOCK_ROWS = 2
BLOCK_COLS = 4


kernel_sigmas = (1.0, 2.5, 6.0)


def extended(block, sides, width):
    for axis, dim in sides:
        count = lax.axis_size(axis)
        forward = [(i, i + 1) for i in range(count - 1)]
        backward = [(target, source) for source, target in forward]
        low = lax.ppermute(
            lax.slice_in_dim(block, block.shape[dim] - width, None, axis=dim), axis, forward
        )
        high = lax.ppermute(lax.slice_in_dim(block, 0, width, axis=dim), axis, backward)
        block = jnp.concatenate([low, block, high], axis=dim)
    return block


def usable_share(bits):
    flagged = jnp.bitwise_and(bits, 6) == 6
    suspect = jnp.bitwise_and(bits, 1).astype(jnp.float32)
    return jnp.where(flagged, 0.0, 1.0 - 0.5 * suspect)


def band_matrix(length, half_span):
    rows_here = jnp.arange(length + 2 * half_span, dtype=jnp.int32)[:, None]
    cols_here = jnp.arange(length, dtype=jnp.int32)[None, :]
    offset = (rows_here - cols_here - half_span).astype(jnp.float32)
    inside = jnp.abs(offset) <= half_span
    taps_axis = jnp.arange(-half_span, half_span + 1).astype(jnp.float32)
    result = []
    for spread in kernel_sigmas:
        norm_sum = jnp.sum(jnp.exp(-taps_axis * taps_axis / (2.0 * spread * spread)))
        result.append(
            jnp.where(inside, jnp.exp(-offset * offset / (2.0 * spread * spread)), 0.0) / norm_sum
        )
    return jnp.stack(result)


def routed(images, mask_bits, inv_var, routes, block_slot, kernel_index, coefficients):
    peer_count = lax.axis_size("exp")
    held_count = images.shape[2]
    capacity = max(2, 2 * held_count // peer_count)
    slot_count = peer_count * capacity
    pixels = BLOCK * BLOCK
    tile_blocks = BLOCK_ROWS * BLOCK_COLS
    coef_count = coefficients.shape[0]
    usable = usable_share(mask_bits[0, 0])
    inverse = inv_var[0, 0][:, None, None]
    weight = (usable * inverse).astype(jnp.bfloat16).reshape(held_count, pixels)
    weighted = (
        (usable * inverse * images[0, 0].astype(jnp.float32))
        .astype(jnp.bfloat16)
        .reshape(held_count, pixels)
    )
    target = routes[0, 0, :, 0]
    ordinal = jnp.arange(held_count, dtype=jnp.int32)
    same_target = target[:, None] == target[None, :]
    earlier = jnp.sum(
        (same_target & (ordinal[None, :] < ordinal[:, None])).astype(jnp.int32), axis=1
    )
    position = target * capacity + earlier
    placed = jnp.arange(slot_count, dtype=jnp.int32)[:, None] == position[None, :]
    placed_int = placed.astype(jnp.int32)
    slot_block = jnp.sum(placed_int * (block_slot[0, 0] + 1)[None, :], axis=1) - 1
    slot_kernel = jnp.sum(placed_int * kernel_index[0, 0][None, :], axis=1)
    labels = jnp.stack([slot_block, slot_kernel], axis=1).reshape(peer_count, capacity, 2)
    placed_half = placed.astype(jnp.bfloat16)
    send_weight = (
        jnp.dot(placed_half, weight, preferred_element_type=jnp.float32)
        .astype(jnp.bfloat16)
        .reshape(peer_count, capacity, pixels)
    )
    block_ids = jnp.arange(tile_blocks, dtype=jnp.int32)[:, None]
    send_weighted = (
        jnp.dot(placed_half, weighted, preferred_element_type=jnp.float32)
        .astype(jnp.bfloat16)
        .reshape(peer_count, capacity, pixels)
    )
    got_weighted, got_weight, got_labels = (
        lax.all_to_all(send_weighted, "exp", split_axis=0, concat_axis=0, tiled=True),
        lax.all_to_all(send_weight, "exp", split_axis=0, concat_axis=0, tiled=True),
        lax.all_to_all(labels, "exp", split_axis=0, concat_axis=0, tiled=True),
    )
    got_labels = got_labels.reshape(slot_count, 2)
    into_block = block_ids == got_labels[:, 0][None, :]
    kernel_pick = (
        got_labels[:, 1][:, None] == jnp.arange(coef_count, dtype=jnp.int32)[None, :]
    ).astype(jnp.float32)
    slot_mix = jnp.dot(kernel_pick, coefficients, precision=lax.Precision.HIGHEST)
    mixing = slot_mix.T[:, None, :] * into_block.astype(jnp.float32)[None, :, :]
    basis_sum = jnp.einsum(
        "kbp,px->kbx",
        mixing,
        got_weighted.reshape(slot_count, pixels).astype(jnp.float32),
        precision=lax.Precision.HIGHEST,
    )
    depth_sum = jnp.dot(
        into_block.astype(jnp.bfloat16),
        got_weight.reshape(slot_count, pixels),
        preferred_element_type=jnp.float32,
    )
    tile_rows = BLOCK_ROWS * BLOCK
    tile_cols = BLOCK_COLS * BLOCK
    basis_tile = (
        basis_sum.reshape(3, BLOCK_ROWS, BLOCK_COLS, BLOCK, BLOCK)
        .transpose(0, 1, 3, 2, 4)
        .reshape(3, tile_rows, tile_cols)
    )
    depth_tile = (
        depth_sum.reshape(BLOCK_ROWS, BLOCK_COLS, BLOCK, BLOCK)
        .transpose(0, 2, 1, 3)
        .reshape(tile_rows, tile_cols)
    )
    half_span = TAPS // 2
    column_mix = band_matrix(tile_cols, half_span)
    row_mix = band_matrix(tile_rows, half_span).transpose(0, 2, 1)
    framed = extended(basis_tile, (("exp", 2), ("tile", 1)), half_span)
    across = jnp.einsum("kyp,kpc->kyc", framed, column_mix, precision=lax.Precision.HIGHEST)
    matched = jnp.einsum("kry,kyc->rc", row_mix, across, precision=lax.Precision.HIGHEST)
    denominator = 1.0 + depth_tile
    coadded = matched / denominator
    detection = lax.psum(coadded * coadded * denominator, "band")
    return (coadded[None], detection)


HALF = TAPS // 2
EDGE = 32
REACH = 24
LINE = 4
PARTS = 4
TILE_BLOCKS = BLOCK_ROWS * BLOCK_COLS
TILE_ROWS = BLOCK_ROWS * BLOCK
TILE_COLS = BLOCK_COLS * BLOCK
MEBI = 1024 * 1024


def tap_values(offset):
    span = np.arange(-HALF, HALF + 1, dtype=np.float64)
    inside = np.abs(offset) <= HALF
    result = []
    for spread in kernel_sigmas:
        total = np.exp(-span * span / (2.0 * spread * spread)).sum()
        value = np.exp(-offset.astype(np.float64) ** 2 / (2.0 * spread * spread)) / total
        result.append(np.where(inside, value, 0.0))
    return np.stack(result)


def split_taps(values):
    high = values.astype(ml_dtypes.bfloat16)
    low = (values - high.astype(np.float64)).astype(ml_dtypes.bfloat16)
    return high, low


def row_taps(target):
    values = tap_values(target[:, None] - np.arange(BLOCK)[None, :])
    return np.concatenate(split_taps(values.reshape(-1, BLOCK)), axis=1)


def tap_scales():
    values = tap_values(np.arange(-HALF, HALF + 1))[:, None, :]
    factors = np.linspace(1.0, 2.0, 4096, endpoint=False)[None, :, None]
    rounded = (values * factors).astype(ml_dtypes.bfloat16).astype(np.float64) / factors
    return factors[0, np.argmin(((rounded - values) ** 2).sum(axis=-1), axis=1), 0]


def column_taps():
    lane = np.arange(BLOCK)
    beside = np.where(lane < BLOCK // 2, lane + BLOCK, lane - BLOCK)
    target = np.concatenate([lane, beside])[None, :]
    values = tap_values(target - lane[:, None]) * tap_scales()[:, None, None]
    rounded = values.reshape(3 * BLOCK, 2 * BLOCK).astype(ml_dtypes.bfloat16)
    return np.concatenate([rounded, rounded], axis=0)


def code(value):
    return (value * jnp.abs(value)).astype(jnp.bfloat16)


def decode(coded):
    square = coded.astype(jnp.float32)
    root = jnp.sqrt(jnp.abs(square))
    return jnp.where(square < 0, -root, root)


def tile_at(place):
    me = lax.axis_index("exp")
    return jnp.where(me < LINE // 2, LINE - 1 - place, place)


def split_rows(block, mixing):
    rows = block.shape[0] // 3
    high, low = [], []
    for k in range(3):
        value = mixing[k] * block[k * rows : (k + 1) * rows]
        rounded = value.astype(jnp.bfloat16)
        high.append(rounded)
        low.append((value - rounded.astype(jnp.float32)).astype(jnp.bfloat16))
    return jnp.concatenate(high + low, axis=1)


def spread_columns(target, column, rows, values):
    beside = values[:, BLOCK:]
    to_right = lax.broadcasted_iota(jnp.int32, beside.shape, 1) < BLOCK // 2
    target[column, rows] += values[:, :BLOCK]
    target[column + 1, rows] += jnp.where(to_right, beside, 0.0)
    target[column - 1, rows] += jnp.where(to_right, 0.0, beside)


def pixel_share(flags, full):
    part = jnp.where((flags & 1) == 1, 0.5 * full, full)
    return jnp.where((flags & 6) == 6, 0.0, part)


def start_all(pairs, sems):
    copies = [pltpu.make_async_copy(src, dst, sems.at[n]) for n, (src, dst) in enumerate(pairs)]
    for copy in copies:
        copy.start()
    return copies


def in_parts(src, dst, parts):
    size = src.shape[0] // parts
    return [(src.at[pl.ds(p * size, size)], dst.at[pl.ds(p * size, size)]) for p in range(parts)]


def depth_kernel(held, *refs):
    routes_in, slots_in, inverse_in, bits_in = refs[:4]
    out_tiles = refs[4 : 4 + LINE]
    routes, slots, inverse, bits, depth, sems = refs[4 + LINE :]
    copies = start_all(
        [(routes_in, routes), (slots_in, slots), (inverse_in, inverse)] + in_parts(bits_in, bits, PARTS),
        sems,
    )
    depth[...] = jnp.zeros_like(depth)
    for copy in copies[:3]:
        copy.wait()
    for s in range(held):
        if s % (held // PARTS) == 0:
            copies[3 + s * PARTS // held].wait()
        weight = pixel_share(bits[s], inverse[s]).astype(jnp.bfloat16)
        depth[routes[s] * TILE_BLOCKS + slots[s]] += weight.astype(jnp.float32)
    for place, ref in enumerate(out_tiles):
        tile = tile_at(place)
        for b in range(TILE_BLOCKS):
            row, col = b // BLOCK_COLS * BLOCK, b % BLOCK_COLS * BLOCK
            ref[row : row + BLOCK, col : col + BLOCK] = depth[tile * TILE_BLOCKS + b].astype(
                jnp.bfloat16
            )


def edge_kernel(held, *refs):
    (
        routes_in, slots_in, kinds_in, inverse_in, coefs_in, bits_in, images_in, taps_in, col_taps_in, passed_in,
        weighted, out_edge, passed,
        routes, slots, kinds, inverse, coefs, bits, images, taps, col_taps, factors, total, sems,
    ) = refs
    strip = lax.axis_index("tile")
    copies = start_all(
        [
            (routes_in, routes), (slots_in, slots), (kinds_in, kinds), (inverse_in, inverse),
            (coefs_in, coefs), (taps_in, taps), (col_taps_in, col_taps),
        ]
        + in_parts(bits_in, bits, PARTS)
        + in_parts(images_in, images, PARTS)
        + [(passed_in, passed)],
        sems,
    )
    total[...] = jnp.zeros_like(total)
    for copy in copies[:6]:
        copy.wait()
    scales = tap_scales()
    for s in range(held):
        if s % (held // PARTS) == 0:
            copies[7 + s * PARTS // held].wait()
            copies[7 + PARTS + s * PARTS // held].wait()
        share = pixel_share(bits[s], inverse[s])
        pixels = (share * images[s].astype(jnp.float32)).astype(jnp.bfloat16)
        weighted[s] = pixels
        moved = jnp.dot(
            taps[1 - strip],
            jnp.concatenate([pixels, pixels], axis=0),
            preferred_element_type=jnp.float32,
        )
        crosses = (slots[s] // BLOCK_COLS == 1 - strip).astype(jnp.float32)
        factors[s * EDGE : (s + 1) * EDGE] = split_rows(
            moved, [crosses * coefs[k, kinds[s]] * float(1.0 / scales[k]) for k in range(3)]
        )
    copies[6].wait()
    copies[-1].wait()
    result = jnp.dot(factors[...], col_taps[...], preferred_element_type=jnp.float32)
    for s in range(held):
        column = 1 + routes[s] * BLOCK_COLS + slots[s] % BLOCK_COLS
        spread_columns(total, column, pl.ds(0, EDGE), result[s * EDGE : (s + 1) * EDGE])
    for place in range(LINE):
        for b in range(BLOCK_COLS):
            out_edge[place, :, b * BLOCK : (b + 1) * BLOCK] = total[
                1 + tile_at(place) * BLOCK_COLS + b
            ].astype(jnp.bfloat16)


def match_kernel(held, ends, *refs):
    pl.when(at_end() == ends)(functools.partial(match_tiles, held, *refs))


def match_tiles(held, *refs):
    routes, slots, kinds, coefs, weighted, taps, col_taps = refs[:7]
    out_tiles = refs[-1 - LINE : -1]
    total = refs[-1]
    total[...] = jnp.zeros_like(total)
    scales = tap_scales()
    size = BLOCK + 2 * REACH
    for start in range(0, held, 4):
        factors = []
        for first in range(start, start + 4, 2):
            both = jnp.concatenate([weighted[first], weighted[first + 1]], axis=1)
            moved = jnp.dot(
                taps[...], jnp.concatenate([both, both], axis=0), preferred_element_type=jnp.float32
            )
            for n in range(2):
                mixing = [coefs[k, kinds[first + n]] * float(1.0 / scales[k]) for k in range(3)]
                factors.append(split_rows(moved[:, n * BLOCK : (n + 1) * BLOCK], mixing))
        result = jnp.dot(
            jnp.concatenate(factors, axis=0), col_taps[...], preferred_element_type=jnp.float32
        )
        for n in range(4):
            slot = slots[start + n]
            row = pl.multiple_of(slot // BLOCK_COLS * BLOCK, 8)
            column = 1 + routes[start + n] * BLOCK_COLS + slot % BLOCK_COLS
            spread_columns(total, column, pl.ds(row, size), result[n * size : (n + 1) * size])
    for place in range(LINE):
        for b in range(BLOCK_COLS):
            out_tiles[place][:, b * BLOCK : (b + 1) * BLOCK] = total[
                1 + tile_at(place) * BLOCK_COLS + b, pl.ds(REACH, TILE_ROWS)
            ]


def edge_rows():
    return pl.ds(pl.multiple_of((1 - lax.axis_index("tile")) * (TILE_ROWS - EDGE), EDGE), EDGE)


def relay_kernel(own, got, edge, *refs):
    out = refs[-2]
    rows = edge_rows()
    out[...] = code(own[...] + decode(got[...]))
    out[rows] = code(own[rows] + edge[...].astype(jnp.float32) + decode(got[rows]))


def plus_kernel(own, got, *refs):
    out = refs[-2]
    out[...] = (own[...].astype(jnp.float32) + got[...].astype(jnp.float32)).astype(jnp.bfloat16)


def add_copy_kernel(own, got, share, _after, out, share_out):
    out[...] = (own[...].astype(jnp.float32) + got[...].astype(jnp.float32)).astype(jnp.bfloat16)
    share_out[...] = share[...]


def at_end():
    me = lax.axis_index("exp")
    return jnp.logical_or(me == 0, me == LINE - 1)


def turn_kernel(third, last, got, _, out, _passed):
    @pl.when(at_end())
    def _():
        out[...] = third[...]

    @pl.when(jnp.logical_not(at_end()))
    def _():
        out[...] = (last[...].astype(jnp.float32) + got[...].astype(jnp.float32)).astype(jnp.bfloat16)


def gather_kernel(
    third_d, last_d, got_d, got_mid_d, third_m, last_m, edge, got_m, out_sum, out_depth, out_inverse
):
    end = at_end()
    rows = edge_rows()
    out_sum[...] = jnp.where(end, last_m[...], third_m[...] + decode(got_m[...]))
    out_sum[rows] += jnp.where(end, edge[3].astype(jnp.float32), edge[2].astype(jnp.float32))
    own_d = jnp.where(end, last_d[...].astype(jnp.float32), third_d[...].astype(jnp.float32))
    denominator = (1.0 + own_d) + got_d[...].astype(jnp.float32) + got_mid_d[...].astype(jnp.float32)
    out_depth[...] = denominator
    out_inverse[...] = 1.0 / denominator


def coadded(matched, inverse, got_mid_m, got_last_m):
    return (matched[...] + decode(jnp.where(at_end(), got_last_m[...], got_mid_m[...]))) * inverse[...]


def term_kernel(matched, depth, inverse, got_mid_m, got_last_m, out_term):
    coadd = coadded(matched, inverse, got_mid_m, got_last_m)
    out_term[...] = (coadd * coadd * depth[...]).astype(jnp.bfloat16)


def coadd_kernel(matched, inverse, got_mid_m, got_last_m, out_coadd):
    out_coadd[...] = coadded(matched, inverse, got_mid_m, got_last_m)


def first_kernel(tile_0, tile_1, tile_2, edge, far, next_far, third):
    rows = edge_rows()
    for place, (source, out) in enumerate(((tile_0, far), (tile_1, next_far), (tile_2, third))):
        out[...] = code(source[...])
        out[rows] = code(source[rows] + edge[place].astype(jnp.float32))


def in_vmem(count):
    return [pl.BlockSpec(memory_space=pltpu.VMEM)] * count


def in_smem(count):
    return [pl.BlockSpec(memory_space=pltpu.SMEM)] * count


def in_hbm(count):
    return [pl.BlockSpec(memory_space=pltpu.HBM)] * count


def vmem_limit(mebibytes):
    return pltpu.CompilerParams(vmem_limit_bytes=mebibytes * MEBI)


def work(microseconds):
    return pl.CostEstimate(
        flops=microseconds * 1_150_000_000, bytes_accessed=0, transcendentals=0
    )


def reduced(images, mask_bits, inv_var, routes, block_slot, kernel_index, coefficients):
    held = images.shape[2]
    tile = jax.ShapeDtypeStruct((TILE_ROWS, TILE_COLS), jnp.bfloat16)
    wide = jax.ShapeDtypeStruct((TILE_ROWS, TILE_COLS), jnp.float32)
    columns = LINE * BLOCK_COLS + 2
    target, slot, kind = routes.reshape(held), block_slot.reshape(held), kernel_index.reshape(held)
    mixing = coefficients.T
    in_place = [pl.BlockSpec(memory_space=pl.ANY)]
    beside = [(0, 1), (1, 0), (2, 3), (3, 2)]
    across = [(1, 2), (2, 1)]

    scalars = [pltpu.SMEM((held,), kind) for kind in (jnp.int32, jnp.int32, jnp.float32)]
    blocks = jax.ShapeDtypeStruct((held, BLOCK, BLOCK), jnp.bfloat16)
    far_d, next_d, third_d, last_d = pl.pallas_call(
        functools.partial(depth_kernel, held),
        out_shape=[tile] * LINE,
        in_specs=in_hbm(4),
        out_specs=in_vmem(LINE),
        scratch_shapes=scalars
        + [
            pltpu.VMEM((held, BLOCK, BLOCK), jnp.int32),
            pltpu.VMEM((LINE * TILE_BLOCKS, BLOCK, BLOCK), jnp.float32),
            pltpu.SemaphoreType.DMA((3 + PARTS,)),
        ],
        compiler_params=vmem_limit(56),
        cost_estimate=work(2),
        name="depth",
    )(target, slot, inv_var.reshape(held), mask_bits[0, 0])
    got_far_d = lax.ppermute(far_d, "exp", [(0, 1), (LINE - 1, LINE - 2)])

    edge_taps = np.stack([row_taps(np.arange(-EDGE, 0)), row_taps(np.arange(BLOCK, BLOCK + EDGE))])
    col_taps = jnp.asarray(column_taps())
    weighted, edge, next_d = pl.pallas_call(
        functools.partial(edge_kernel, held),
        out_shape=[blocks, jax.ShapeDtypeStruct((LINE, EDGE, TILE_COLS), jnp.bfloat16), tile],
        in_specs=in_hbm(10),
        out_specs=in_vmem(3),
        scratch_shapes=[pltpu.SMEM((held,), jnp.int32)]
        + scalars
        + [
            pltpu.SMEM(mixing.shape, jnp.float32),
            pltpu.VMEM((held, BLOCK, BLOCK), jnp.int32),
            pltpu.VMEM((held, BLOCK, BLOCK), jnp.bfloat16),
            pltpu.VMEM(edge_taps.shape, jnp.bfloat16),
            pltpu.VMEM(col_taps.shape, jnp.bfloat16),
            pltpu.VMEM((held * EDGE, 6 * BLOCK), jnp.bfloat16),
            pltpu.VMEM((columns, EDGE, BLOCK), jnp.float32),
            pltpu.SemaphoreType.DMA((8 + 2 * PARTS,)),
        ],
        compiler_params=vmem_limit(24),
        cost_estimate=work(3),
        name="edges",
    )(
        target, slot, kind, inv_var.reshape(held), mixing, mask_bits[0, 0], images[0, 0],
        jnp.asarray(edge_taps), col_taps, next_d,
    )
    other_edge = lax.ppermute(edge, "tile", [(0, 1), (1, 0)])
    got_next_d = lax.ppermute(next_d, "exp", [(0, 1), (LINE - 1, LINE - 2)])
    own_rows = jnp.asarray(row_taps(np.arange(-REACH, BLOCK + REACH)))

    def match(ends, after):
        return pl.pallas_call(
            functools.partial(match_kernel, held, ends),
            out_shape=[wide] * LINE,
            in_specs=in_smem(4) + in_vmem(3) + in_place * len(after),
            out_specs=in_vmem(LINE),
            scratch_shapes=[pltpu.VMEM((columns, TILE_ROWS + 2 * REACH, BLOCK), jnp.float32)],
            compiler_params=vmem_limit(24),
            cost_estimate=work(0),
            name="match",
        )(target, slot, kind, mixing, weighted, own_rows, col_taps, *after)

    end_tiles = match(True, [])
    far_m, next_m, third_m = pl.pallas_call(
        first_kernel,
        out_shape=[tile, tile, tile],
        in_specs=in_vmem(4),
        out_specs=in_vmem(3),
        compiler_params=vmem_limit(24),
        cost_estimate=work(0),
        name="first",
    )(*end_tiles[:3], other_edge)

    def passing(kernel, name, operands, after, passed):
        return pl.pallas_call(
            kernel,
            out_shape=[tile, jax.ShapeDtypeStruct(passed.shape, passed.dtype)],
            in_specs=in_vmem(len(operands)) + in_place * (len(after) + 1),
            out_specs=in_vmem(1) + in_place,
            input_output_aliases={len(operands) + len(after): 1},
            compiler_params=vmem_limit(24),
            cost_estimate=work(1),
            name=name,
        )(*operands, *after, passed)

    nothing = jnp.zeros((8, 128), jnp.float32)
    got_far_m = lax.ppermute(far_m, "exp", [(0, 1), (LINE - 1, LINE - 2)])
    far_sum, next_m = passing(plus_kernel, "plus", [far_d, got_far_d], [], next_m)
    mid_far_d = lax.ppermute(far_sum, "exp", across)
    mid_tiles = match(False, [far_sum])
    next_sum, next_m = pl.pallas_call(
        add_copy_kernel,
        out_shape=[tile, tile],
        in_specs=in_vmem(3) + in_place,
        out_specs=in_vmem(2),
        compiler_params=vmem_limit(24),
        cost_estimate=work(1),
        name="plus",
    )(next_d, got_next_d, next_m, mid_tiles[0])
    got_next_m = lax.ppermute(next_m, "exp", beside)
    mid_d = lax.ppermute(next_sum, "exp", across)
    far_relayed, third_m = passing(
        relay_kernel, "relay", [mid_tiles[0], got_far_m, other_edge[0]], [mid_far_d], third_m
    )
    mid_far_m = lax.ppermute(far_relayed, "exp", across)
    turned, _ = passing(turn_kernel, "turn", [third_d, last_d, mid_far_d], [], nothing)
    got_d = lax.ppermute(turned, "exp", beside)
    next_relayed, third_m = passing(
        relay_kernel, "relay", [mid_tiles[1], got_next_m, other_edge[1]], [], third_m
    )
    mid_m = lax.ppermute(next_relayed, "exp", across)
    got_m = lax.ppermute(third_m, "exp", [(0, 1), (LINE - 1, LINE - 2)])
    last_relayed, _ = passing(
        relay_kernel, "relay", [mid_tiles[3], mid_far_m, other_edge[3]], [got_d, mid_d], nothing
    )
    end_m = lax.ppermute(last_relayed, "exp", [(1, 0), (LINE - 2, LINE - 1)])
    matched, depth, inverse = pl.pallas_call(
        gather_kernel,
        out_shape=[wide] * 3,
        in_specs=in_vmem(8),
        out_specs=in_vmem(3),
        compiler_params=vmem_limit(24),
        cost_estimate=work(1),
        name="gather",
    )(third_d, last_d, got_d, mid_d, mid_tiles[2], end_tiles[3], other_edge, got_m)

    def ending(kernel, name, shape, *operands):
        return pl.pallas_call(
            kernel,
            out_shape=shape,
            in_specs=in_vmem(len(operands)),
            out_specs=pl.BlockSpec(memory_space=pltpu.VMEM),
            compiler_params=vmem_limit(24),
            cost_estimate=work(1),
            name=name,
        )(*operands)

    term = ending(term_kernel, "term", tile, matched, depth, inverse, mid_m, end_m)
    coadd = ending(coadd_kernel, "coadd", wide, matched, inverse, mid_m, end_m)
    other_term = lax.ppermute(term, "band", [(0, 1), (1, 0)])
    detection = term.astype(jnp.float32) + other_term.astype(jnp.float32)
    return (coadd[None], detection)


def local(images, mask_bits, inv_var, routes, block_slot, kernel_index, coefficients):
    peers = lax.axis_size("exp")
    partial_sums_fit = peers * TILE_BLOCKS <= 2 * images.shape[2]
    pairs = lax.axis_size("tile") == 2 and lax.axis_size("band") == 2
    plan = reduced if partial_sums_fit and pairs and peers == LINE else routed
    return plan(images, mask_bits, inv_var, routes, block_slot, kernel_index, coefficients)


def solution(mesh):
    return jax.shard_map(
        local,
        mesh=mesh,
        in_specs=(
            P(("patch", "band"), "tile", "exp", None, None),
            P(("patch", "band"), "tile", "exp", None, None),
            P(("patch", "band"), "tile", "exp"),
            P(("patch", "band"), "tile", "exp", None),
            P(("patch", "band"), "tile", "exp"),
            P(("patch", "band"), "tile", "exp"),
            P(),
        ),
        out_specs=(P(("patch", "band"), "tile", "exp"), P(("patch", "tile"), "exp")),
        check_vma=False,
    )
```
